32 devices in a mesh: sec: 4 (over x, core), rows: 8 (over z, y).
Axes of the slice: x: 2, y: 2, z: 4, core: 2. Of those that a mesh axis runs over, the one named last changes fastest.
Arguments:
- streams: bfloat16 [4, 2, 16, 64, 256], P('sec', None, 'rows'), may hold values from -6 to 6
- cotangents: bfloat16 [4, 2, 16, 64, 256], P('sec', None, 'rows'), may hold values from -6 to 6
- weights: bfloat16 [4, 1, 2, 3, 3, 256, 256], P('sec'), may hold values from -0.125 to 0.125
Outputs:
- input_streams: bfloat16 [4, 2, 16, 64, 256], P('sec', None, 'rows')
- input_grads: bfloat16 [4, 2, 16, 64, 256], P('sec', None, 'rows')
- weight_grads: float32 [4, 4608, 256], P('sec', 'rows')
The draws below stay inside these ranges and needn't reach their ends.
All inputs are finite; a program needn't handle non-finite values.
Results may differ from the reference program's by a relative error of at most 0.019.
Values may be sent and summed in bfloat16 or wider, within the bound.
A program may use at most 64 MiB of HBM per device.

```python
import jax
import jax.numpy as jnp
from jax import lax

C = 256
LAYERS = 1
WIDTH = 64
SECTIONS = 4
CROPS = 4
HEIGHT = 16
N_SEC = 4


def levels(rng, shape, pieces, low, top_value):
    factor_of, own = 1.0, jax.random.fold_in(rng, 6)
    for dim, parts in pieces:
        heights = jnp.exp(jax.random.uniform(jax.random.fold_in(own, dim), (parts,), jnp.float32, low / len(pieces), top_value / len(pieces)))
        factor_of = factor_of * jnp.repeat(heights, shape[dim] // parts).reshape([-1 if axis == dim else 1 for axis in range(len(shape))])
    return factor_of


def centred(own_key, dims, spread, bound, shards=(), kind=jnp.bfloat16):
    values = spread * jax.random.normal(own_key, dims, jnp.float32)
    if shards:
        values = values * levels(own_key, dims, shards, -0.22, 0.18)
    return jnp.clip(values, -bound, bound).astype(kind)


def setup_inputs(seed: int = 0) -> dict:
    key_of = jax.random.split(jax.random.key(seed), 4)
    streams = centred(key_of[0], (CROPS, 2, HEIGHT, WIDTH, C), 1.0, 6.0, ((0, 4), (2, 8)))
    cotangents = centred(key_of[1], (CROPS, 2, HEIGHT, WIDTH, C), 1.0, 6.0, ((0, 4), (2, 8)))
    weights = centred(key_of[2], (SECTIONS, LAYERS, 2, 3, 3, C, C), (9 * C) ** -0.5, 0.125, ((0, 4),))
    return {"streams": streams, "cotangents": cotangents, "weights": weights}


def conv_same(field, kernel):
    return lax.conv_general_dilated(field.astype(jnp.float32)[None], kernel.astype(jnp.float32), (1, 1), ((1, 1), (1, 1)), dimension_numbers=("NHWC", "HWIO", "NHWC"), precision=lax.Precision.HIGHEST)[0]


def turn_kernel(kernel):
    return jnp.flip(kernel, (0, 1)).swapaxes(2, 3)


def silu_slope(value):
    sig = jax.nn.sigmoid(value)
    return sig + value * sig * (1.0 - sig)


def tap_grads(act, cotan):
    padded = jnp.pad(act.astype(jnp.float32), ((1, 1), (1, 1), (0, 0)))
    height, width = cotan.shape[0], cotan.shape[1]
    patches = jnp.stack([padded[row_tap:row_tap + height, col_tap:col_tap + width] for row_tap in range(3) for col_tap in range(3)])
    summed = jnp.einsum("khwi,hwo->kio", patches, cotan.astype(jnp.float32), precision=lax.Precision.HIGHEST)
    return summed.reshape(3, 3, act.shape[-1], cotan.shape[-1])


def layer_back(state, kernel_f, kernel_g):
    upper = state[0].astype(jnp.float32)
    act_g = jax.nn.silu(upper).astype(jnp.bfloat16)
    lower_in = (state[1].astype(jnp.float32) - conv_same(act_g, kernel_g)).astype(jnp.bfloat16)
    carried = (state[2].astype(jnp.float32) + conv_same(state[3], turn_kernel(kernel_g)) * silu_slope(upper)).astype(jnp.bfloat16)
    grad_g = tap_grads(act_g, state[3])
    lower_wide = lower_in.astype(jnp.float32)
    act_f = jax.nn.silu(lower_wide).astype(jnp.bfloat16)
    upper_in = (upper - conv_same(act_f, kernel_f)).astype(jnp.bfloat16)
    grad_lower_in = (state[3].astype(jnp.float32) + conv_same(carried, turn_kernel(kernel_f)) * silu_slope(lower_wide)).astype(jnp.bfloat16)
    grad_f = tap_grads(act_f, carried)
    return jnp.stack([upper_in, lower_in, carried, grad_lower_in]), grad_f, grad_g


def reference(streams, cotangents, weights):
    grads = jnp.zeros((N_SEC, LAYERS, 2, 3, 3, C, C), jnp.float32)
    results = []
    for crop in range(CROPS):
        state = jnp.concatenate([streams[crop], cotangents[crop]], 0)
        for section in reversed(range(N_SEC)):
            for layer in reversed(range(LAYERS)):
                state, grad_f, grad_g = layer_back(state, weights[section, layer, 0], weights[section, layer, 1])
                grads = grads.at[section, layer, 0].add(grad_f)
                grads = grads.at[section, layer, 1].add(grad_g)
        results.append(state)
    finished = jnp.stack(results)
    scale = (CROPS * HEIGHT * WIDTH) ** -0.5
    weight_grads = (grads * scale).reshape(N_SEC, LAYERS * 18 * C, C)
    return finished[:, :2], finished[:, 2:], weight_grads
```

```python
import functools

import jax
import jax.numpy as jnp
from jax import lax
from jax.experimental import pallas as pl
from jax.experimental.pallas import tpu as pltpu
from jax.sharding import PartitionSpec as P

MESH = pl.DeviceIdType.MESH
F32 = jnp.float32
BF16 = jnp.bfloat16


def silu_slope(value):
    sig = jax.nn.sigmoid(value)
    return sig + value * sig * (1.0 - sig)


def shift_cols(value, by, width):
    pixels = value.shape[0]
    col = lax.rem(lax.broadcasted_iota(jnp.int32, value.shape, 0), width)
    rolled = pltpu.roll(value, by % pixels, axis=0)
    edge = 0 if by > 0 else width - 1
    return jnp.where(col == edge, 0.0, rolled)


def conv(field, kernel_ref, which, width, turned):
    pixels = field.shape[0] - 2 * width
    dims = (((1,), (1 if turned else 0,)), ((), ()))
    parts = []
    for b in range(3):
        total = None
        for a in range(3):
            tap = kernel_ref[which, 2 - a, 2 - b] if turned else kernel_ref[which, a, b]
            term = lax.dot_general(
                field[a * width : a * width + pixels], tap, dims, preferred_element_type=F32
            )
            total = term if total is None else total + term
        parts.append(total)
    return parts[1] + shift_cols(parts[0], 1, width) + shift_cols(parts[2], -1, width)


def add_grads(acc_ref, which, field, cotan, width):
    pixels, channels = cotan.shape
    wide = cotan.astype(F32)
    shifted = jnp.concatenate(
        [
            shift_cols(wide, -1, width).astype(BF16),
            cotan,
            shift_cols(wide, 1, width).astype(BF16),
        ],
        axis=1,
    )
    for a in range(3):
        term = lax.dot_general(
            field[a * width : a * width + pixels],
            shifted,
            (((0,), (0,)), ((), ())),
            preferred_element_type=F32,
        )
        for b in range(3):
            start = ((which * 3 + a) * 3 + b) * channels
            acc_ref[start : start + channels] += term[:, b * channels : (b + 1) * channels]


def body(
    S, N, scale,
    streams, cotangents, weights, out_streams, out_grads, out_weights,
    first, first_edge, state, made, edge_a, made_a, edge_b, made_b, result, acc, terms, got,
    first_send, st_send, st_recv, ea_send, ea_recv, eb_send, eb_recv,
    res_send, res_recv, rs_send, rs_recv,
):
    s, r = lax.axis_index("sec"), lax.axis_index("rows")
    M = S
    rows, width, channels = state.shape[2:]
    chunk = terms.shape[1]
    last_sec = s == S - 1
    below, above = lax.rem(r + 1, N), lax.rem(r + N - 1, N)
    has_above, has_below = r > 0, r < N - 1
    sides = ((0, above, has_above), (1, below, has_below))
    lower_sec = lax.rem(s + S - 1, S)

    def remote(src, dst, send, recv, sec, row):
        return pltpu.make_async_remote_copy(
            src_ref=src, dst_ref=dst, send_sem=send, recv_sem=recv,
            device_id=(sec, row), device_id_type=MESH,
        )

    barrier = pltpu.get_barrier_semaphore()
    for step in range(S):
        sec = lax.rem(s + step, S)
        if step > 0:
            pl.semaphore_signal(barrier, inc=1, device_id=(sec, r), device_id_type=MESH)
        for _, row, there in sides:
            if step > 0:
                @pl.when(there)
                def _(sec=sec, row=row):
                    pl.semaphore_signal(barrier, inc=1, device_id=(sec, row), device_id_type=MESH)
    for step in range(1, N):
        pl.semaphore_signal(
            barrier, inc=1, device_id=(s, lax.rem(r + step, N)), device_id_type=MESH
        )

    own = S - 1 - s
    first[0] = streams[0, 0]
    first[1] = cotangents[0, 1]
    first[2] = streams[0, 1]
    first[3] = cotangents[0, 0]
    for side in range(2):
        row = 0 if side == 0 else rows - 1
        first_edge[side, 0] = streams[0, 0, row]
        first_edge[side, 1] = cotangents[0, 1, row]

    @pl.when(last_sec)
    def _():
        state[0] = first[...]

    for side, _, there in sides:
        @pl.when(jnp.logical_not(there))
        def _(side=side):
            edge_a[:, side] = jnp.zeros(edge_a.shape[:1] + edge_a.shape[2:], BF16)
            edge_b[:, side] = jnp.zeros(edge_b.shape[:1] + edge_b.shape[2:], BF16)

    near = 1 + has_above.astype(jnp.int32) + has_below.astype(jnp.int32)
    pl.semaphore_wait(barrier, (S - 1) * near + N - 1)

    def first_edges(side, row):
        return remote(
            first_edge.at[side], edge_a.at[own, 1 - side],
            first_send.at[2 + side], ea_recv.at[own, 1 - side], S - 1, row,
        )

    def first_states(half):
        return remote(
            first.at[pl.ds(2 * half, 2)], state.at[own, pl.ds(2 * half, 2)],
            first_send.at[half], st_recv.at[own, half], S - 1, r,
        )

    for side, row, there in sides:
        @pl.when(there)
        def _(side=side, row=row):
            first_edges(side, row).start()

    @pl.when(jnp.logical_not(last_sec))
    def _():
        for half in range(2):
            first_states(half).start()

    acc[...] = jnp.zeros(acc.shape, F32)

    def state_copy(m, half):
        return remote(
            made.at[m, pl.ds(2 * half, 2)], state.at[m, pl.ds(2 * half, 2)],
            st_send.at[m, half], st_recv.at[m, half], lower_sec, r,
        )

    def result_copy(m, half):
        return remote(
            made.at[m, pl.ds(2 * half, 2)], result.at[pl.ds(2 * half, 2)],
            res_send.at[m, half], res_recv.at[half], S - 1 - m, r,
        )

    def edge_a_copy(m, side, row):
        return remote(
            made_a.at[m, side], edge_a.at[m, 1 - side],
            ea_send.at[m, side], ea_recv.at[m, 1 - side], lower_sec, row,
        )

    def edge_b_copy(m, side, row):
        return remote(
            made_b.at[m, side], edge_b.at[m, 1 - side],
            eb_send.at[m, side], eb_recv.at[m, 1 - side], s, row,
        )

    def send_half(m, half):
        @pl.when(s > 0)
        def _():
            state_copy(m, half).start()

        @pl.when((s == 0) & (m < M - 1))
        def _():
            result_copy(m, half).start()

    def term_copy(p):
        return remote(terms.at[p], got.at[r], rs_send.at[p], rs_recv.at[r], s, p)

    def send_terms(low, count):
        def one(i, carry):
            p = low + lax.rem(r + 1 + i, count)
            @pl.when(p != r)
            def _():
                start = pl.multiple_of(p * chunk, chunk)
                terms[p] = acc[pl.ds(start, chunk)].astype(terms.dtype)
                term_copy(p).start()
            return carry
        lax.fori_loop(0, count, one, 0)

    def flat(value):
        return value.reshape(-1, channels)

    def step(m, carry):
        for side, row, there in sides:
            @pl.when(there)
            def _(side=side, row=row):
                edge_a_copy(m, 1 - side, row).wait_recv()

        arrives = jnp.logical_not(last_sec & (m == 0))

        @pl.when(arrives)
        def _():
            state_copy(m, 0).wait_recv()
            state_copy(m, 1).wait_recv()

        y1 = flat(state[m, 0]).astype(F32)
        g2 = flat(state[m, 1])
        upper = jnp.concatenate([edge_a[m, 0, 0], flat(state[m, 0]), edge_a[m, 1, 0]], 0)
        act_g = jax.nn.silu(upper.astype(F32)).astype(BF16)
        g2_wide = jnp.concatenate([edge_a[m, 0, 1], g2, edge_a[m, 1, 1]], 0)
        x2 = (flat(state[m, 2]).astype(F32) - conv(act_g, weights, 1, width, False)).astype(BF16)
        carried = (
            flat(state[m, 3]).astype(F32)
            + conv(g2_wide, weights, 1, width, True) * silu_slope(y1)
        ).astype(BF16)
        made_b[m, 0, 0] = x2[:width]
        made_b[m, 0, 1] = carried[:width]
        made_b[m, 1, 0] = x2[-width:]
        made_b[m, 1, 1] = carried[-width:]
        for side, row, there in sides:
            @pl.when(there)
            def _(side=side, row=row):
                edge_b_copy(m, side, row).start()
        made[m, 2] = x2.reshape(rows, width, channels)
        made[m, 3] = carried.reshape(rows, width, channels)
        send_half(m, 1)

        add_grads(acc, 1, act_g, g2, width)

        @pl.when(m == M - 1)
        def _():
            send_terms(N // 2, N - N // 2)

        for side, row, there in sides:
            @pl.when(there)
            def _(side=side, row=row):
                edge_b_copy(m, 1 - side, row).wait_recv()
        lower = jnp.concatenate([edge_b[m, 0, 0], x2, edge_b[m, 1, 0]], 0)
        act_f = jax.nn.silu(lower.astype(F32)).astype(BF16)
        carried_wide = jnp.concatenate([edge_b[m, 0, 1], carried, edge_b[m, 1, 1]], 0)
        x1 = (y1 - conv(act_f, weights, 0, width, False)).astype(BF16)
        gx2 = (
            g2.astype(F32)
            + conv(carried_wide, weights, 0, width, True) * silu_slope(x2.astype(F32))
        ).astype(BF16)
        made_a[m, 0, 0] = x1[:width]
        made_a[m, 0, 1] = gx2[:width]
        made_a[m, 1, 0] = x1[-width:]
        made_a[m, 1, 1] = gx2[-width:]
        for side, row, there in sides:
            @pl.when(there & (s > 0))
            def _(side=side, row=row):
                edge_a_copy(m, side, row).start()
        made[m, 0] = x1.reshape(rows, width, channels)
        made[m, 1] = gx2.reshape(rows, width, channels)
        send_half(m, 0)

        add_grads(acc, 0, act_f, carried, width)
        return carry

    lax.fori_loop(0, M, step, 0)
    send_terms(0, N // 2)

    def deliver(source):
        out_streams[0, 0] = source[0]
        out_grads[0, 1] = source[1]
        out_streams[0, 1] = source[2]
        out_grads[0, 0] = source[3]

    @pl.when(s == 0)
    def _():
        deliver(made[M - 1])

    @pl.when(s > 0)
    def _():
        result_copy(0, 0).wait_recv()
        result_copy(0, 1).wait_recv()
        deliver(result[...])

    out_weights[0] = acc[pl.ds(pl.multiple_of(r * chunk, chunk), chunk)] * scale

    def gather(i, carry):
        p = lax.rem(r + i, N)
        remote(terms.at[p], got.at[p], rs_send.at[p], rs_recv.at[p], s, p).wait_recv()
        out_weights[0] += got[p].astype(F32) * scale
        return carry

    lax.fori_loop(1, N, gather, 0)

    for side, row, there in sides:
        @pl.when(there)
        def _(side=side, row=row):
            first_edges(side, row).wait_send()

    @pl.when(jnp.logical_not(last_sec))
    def _():
        for half in range(2):
            first_states(half).wait_send()

    def drain(m, carry):
        for side, row, there in sides:
            @pl.when(there)
            def _(side=side, row=row):
                edge_b_copy(m, side, row).wait_send()

            @pl.when(there & (s > 0))
            def _(side=side, row=row):
                edge_a_copy(m, side, row).wait_send()

        for half in range(2):
            @pl.when(s > 0)
            def _(half=half):
                state_copy(m, half).wait_send()

            @pl.when((s == 0) & (m < M - 1))
            def _(half=half):
                result_copy(m, half).wait_send()
        return carry

    lax.fori_loop(0, M, drain, 0)

    def drain_terms(i, carry):
        term_copy(lax.rem(r + i, N)).wait_send()
        return carry

    lax.fori_loop(1, N, drain_terms, 0)


def local(S, N, streams, cotangents, weights):
    mine, _, rows, width, channels = streams.shape
    layers = weights.shape[1]
    assert mine == 1 and layers == 1 and N % 2 == 0
    M = S
    scale = (M * rows * N * width) ** -0.5
    total = 18 * channels
    chunk = total // N
    sent = BF16 if chunk % 16 == 0 else F32
    dma = pltpu.SemaphoreType.DMA
    vmem = pl.BlockSpec(memory_space=pltpu.VMEM)
    shard = (rows, width, channels)
    edge = (2, 2, width, channels)
    return pl.pallas_call(
        functools.partial(body, S, N, scale),
        out_shape=(
            jax.ShapeDtypeStruct(streams.shape, BF16),
            jax.ShapeDtypeStruct(streams.shape, BF16),
            jax.ShapeDtypeStruct((1, chunk, channels), F32),
        ),
        in_specs=[vmem] * 3,
        out_specs=(vmem,) * 3,
        scratch_shapes=[
            pltpu.VMEM((4,) + shard, BF16),
            pltpu.VMEM(edge, BF16),
            pltpu.VMEM((M, 4) + shard, BF16),
            pltpu.VMEM((M, 4) + shard, BF16),
            pltpu.VMEM((M,) + edge, BF16),
            pltpu.VMEM((M,) + edge, BF16),
            pltpu.VMEM((M,) + edge, BF16),
            pltpu.VMEM((M,) + edge, BF16),
            pltpu.VMEM((4,) + shard, BF16),
            pltpu.VMEM((total, channels), F32),
            pltpu.VMEM((N, chunk, channels), sent),
            pltpu.VMEM((N, chunk, channels), sent),
            dma((4,)),
            dma((M, 2)), dma((M, 2)), dma((M, 2)), dma((M, 2)), dma((M, 2)), dma((M, 2)),
            dma((M, 2)), dma((2,)), dma((N,)), dma((N,)),
        ],
        compiler_params=pltpu.CompilerParams(
            collective_id=0, has_side_effects=True, vmem_limit_bytes=40 * 1024 * 1024
        ),
        cost_estimate=pl.CostEstimate(
            flops=M * 108 * rows * width * channels * channels,
            bytes_accessed=weights.size * 2,
            transcendentals=0,
        ),
    )(streams, cotangents, weights[0, 0])


def solution(mesh):
    placed = (
        P("sec", None, "rows", None, None),
        P("sec", None, "rows", None, None),
        P("sec", None, None, None, None, None, None),
    )
    return jax.shard_map(
        functools.partial(local, mesh.shape["sec"], mesh.shape["rows"]),
        mesh=mesh,
        in_specs=placed,
        out_specs=(
            P("sec", None, "rows", None, None),
            P("sec", None, "rows", None, None),
            P("sec", "rows", None),
        ),
        check_vma=False,
    )
```

```python
import functools

import jax
import jax.numpy as jnp
from jax import lax
from jax.experimental import pallas as pl
from jax.experimental.pallas import tpu as pltpu
from jax.sharding import PartitionSpec as P

MESH = pl.DeviceIdType.MESH
F32 = jnp.float32
BF16 = jnp.bfloat16


def silu_slope(value):
    sig = jax.nn.sigmoid(value)
    return sig + value * sig * (1.0 - sig)


def shift_cols(value, by, width):
    pixels = value.shape[0]
    col = lax.rem(lax.broadcasted_iota(jnp.int32, value.shape, 0), width)
    rolled = pltpu.roll(value, by % pixels, axis=0)
    edge = 0 if by > 0 else width - 1
    return jnp.where(col == edge, 0.0, rolled)


def conv(field, kernel_ref, which, width, turned):
    pixels = field.shape[0] - 2 * width
    dims = (((1,), (1 if turned else 0,)), ((), ()))
    parts = []
    for b in range(3):
        total = None
        for a in range(3):
            tap = kernel_ref[which, 2 - a, 2 - b] if turned else kernel_ref[which, a, b]
            term = lax.dot_general(
                field[a * width : a * width + pixels], tap, dims, preferred_element_type=F32
            )
            total = term if total is None else total + term
        parts.append(total)
    return parts[1] + shift_cols(parts[0], 1, width) + shift_cols(parts[2], -1, width)


def add_grads(acc_ref, which, field, cotan, width):
    pixels, channels = cotan.shape
    wide = cotan.astype(F32)
    shifted = jnp.concatenate(
        [
            shift_cols(wide, -1, width).astype(BF16),
            cotan,
            shift_cols(wide, 1, width).astype(BF16),
        ],
        axis=1,
    )
    for a in range(3):
        term = lax.dot_general(
            field[a * width : a * width + pixels],
            shifted,
            (((0,), (0,)), ((), ())),
            preferred_element_type=F32,
        )
        for b in range(3):
            start = ((which * 3 + a) * 3 + b) * channels
            acc_ref[start : start + channels] += term[:, b * channels : (b + 1) * channels]


def body(
    S, N, scale,
    streams, cotangents, weights_in, out_streams, out_grads, out_weights,
    weights, first, state, made, edge_a, edge_b, result, acc, terms, mid, sums, got,
    in_sem, w_sem, first_send, fedge_send, st_send, st_recv, ea_send, ea_recv, eb_send, eb_recv,
    res_send, res_recv, pair_send, pair_recv, rs_send, rs_recv,
):
    s, r = lax.axis_index("sec"), lax.axis_index("rows")
    M = S
    rows, width, channels = state.shape[2:]
    chunk = terms.shape[1]
    last_sec = s == S - 1
    below, above = lax.rem(r + 1, N), lax.rem(r + N - 1, N)
    has_above, has_below = r > 0, r < N - 1
    sides = ((0, above, has_above), (1, below, has_below))
    edge_row = (0, rows - 1)
    lower_sec = lax.rem(s + S - 1, S)
    half, group = lax.rem(r, 2), r // 2
    groups = N // 2
    partner = 2 * group + 1 - half

    def remote(src, dst, send, recv, sec, row):
        return pltpu.make_async_remote_copy(
            src_ref=src, dst_ref=dst, send_sem=send, recv_sem=recv,
            device_id=(sec, row), device_id_type=MESH,
        )

    own = S - 1 - s
    sources = (streams.at[0, 0], cotangents.at[0, 1], streams.at[0, 1], cotangents.at[0, 0])
    loads = [pltpu.make_async_copy(src, first.at[i], in_sem.at[i]) for i, src in enumerate(sources)]
    for load in loads:
        load.start()
    kernel_loads = [
        pltpu.make_async_copy(weights_in.at[0, 0, i], weights.at[i], w_sem.at[i]) for i in (1, 0)
    ]
    for load in kernel_loads:
        load.start()

    barrier = pltpu.get_barrier_semaphore()
    for step in range(S):
        sec = lax.rem(s + step, S)
        if step > 0:
            pl.semaphore_signal(barrier, inc=1, device_id=(sec, r), device_id_type=MESH)
        for _, row, there in sides:
            if step > 0:
                @pl.when(there)
                def _(sec=sec, row=row):
                    pl.semaphore_signal(barrier, inc=1, device_id=(sec, row), device_id_type=MESH)
    for step in range(1, N):
        pl.semaphore_signal(
            barrier, inc=1, device_id=(s, lax.rem(r + step, N)), device_id_type=MESH
        )

    for side, _, there in sides:
        @pl.when(jnp.logical_not(there))
        def _(side=side):
            edge_a[:, side] = jnp.zeros(edge_a.shape[:1] + edge_a.shape[2:], BF16)
            edge_b[:, side] = jnp.zeros(edge_b.shape[:1] + edge_b.shape[2:], BF16)

    for load in loads:
        load.wait()

    @pl.when(last_sec)
    def _():
        state[0] = first[...]

    near = 1 + has_above.astype(jnp.int32) + has_below.astype(jnp.int32)
    pl.semaphore_wait(barrier, (S - 1) * near + N - 1)

    def first_edge(i, side, row):
        return remote(
            first.at[i, edge_row[side]], edge_a.at[own, 1 - side, i],
            fedge_send.at[side, i], ea_recv.at[own, 2 * (1 - side) + i], S - 1, row,
        )

    def first_state(i):
        return remote(
            first.at[i], state.at[own, i], first_send.at[i], st_recv.at[own, i], S - 1, r,
        )

    for i in range(2):
        for side, row, there in sides:
            @pl.when(there)
            def _(i=i, side=side, row=row):
                first_edge(i, side, row).start()

    @pl.when(jnp.logical_not(last_sec))
    def _():
        for i in range(4):
            first_state(i).start()

    acc[...] = jnp.zeros(acc.shape, F32)
    for load in kernel_loads:
        load.wait()

    def state_copy(m, i):
        return remote(
            made.at[m, i], state.at[m, i], st_send.at[m, i], st_recv.at[m, i], lower_sec, r,
        )

    def result_copy(m, i):
        return remote(
            made.at[m, i], result.at[i], res_send.at[m, i], res_recv.at[i], S - 1 - m, r,
        )

    def edge_a_copy(m, i, side, row):
        return remote(
            made.at[m, i, edge_row[side]], edge_a.at[m, 1 - side, i],
            ea_send.at[m, 2 * side + i], ea_recv.at[m, 2 * (1 - side) + i], lower_sec, row,
        )

    def edge_b_copy(m, i, side, row):
        return remote(
            made.at[m, 2 + i, edge_row[side]], edge_b.at[m, 1 - side, i],
            eb_send.at[m, 2 * side + i], eb_recv.at[m, 2 * (1 - side) + i], s, row,
        )

    def send_on(m, i):
        @pl.when(s > 0)
        def _():
            state_copy(m, i).start()

        @pl.when((s == 0) & (m < M - 1))
        def _():
            result_copy(m, i).start()

    def rows_of(p):
        return pl.ds(pl.multiple_of(p * chunk, chunk), chunk)

    def pair_copy(k):
        return remote(terms.at[k], mid.at[k], pair_send.at[k], pair_recv.at[k], s, partner)

    def sum_copy(k):
        return remote(
            sums.at[k], got.at[group], rs_send.at[k], rs_recv.at[group], s, 2 * k + half
        )

    def send_pairs(low, count):
        def one(i, carry):
            k = low + lax.rem(group + 1 + i, count)
            terms[k] = acc[rows_of(2 * k + 1 - half)].astype(terms.dtype)
            pair_copy(k).start()
            return carry
        lax.fori_loop(0, count, one, 0)

    def send_sums(low, count):
        def one(i, carry):
            k = low + lax.rem(group + 1 + i, count)
            pair_copy(k).wait_recv()
            total = acc[rows_of(2 * k + half)] + mid[k].astype(F32)

            @pl.when(k == group)
            def _():
                out_weights[0] = total

            @pl.when(k != group)
            def _():
                sums[k] = total.astype(sums.dtype)
                sum_copy(k).start()
            return carry
        lax.fori_loop(0, count, one, 0)

    def flat(value):
        return value.reshape(-1, channels)

    def step(m, carry):
        arrives = jnp.logical_not(last_sec & (m == 0))

        def await_state(i):
            @pl.when(arrives)
            def _():
                state_copy(m, i).wait_recv()

        def await_edges(copy, i):
            for side, row, there in sides:
                @pl.when(there)
                def _(side=side, row=row):
                    copy(m, i, 1 - side, row).wait_recv()

        def send_edges(copy, i, ok=True):
            for side, row, there in sides:
                @pl.when(there & ok)
                def _(side=side, row=row):
                    copy(m, i, side, row).start()

        def grads_g():
            add_grads(acc, 1, act_g, g2, width)

        await_edges(edge_a_copy, 0)
        await_state(0)
        y1 = flat(state[m, 0])
        upper = jnp.concatenate([edge_a[m, 0, 0], y1, edge_a[m, 1, 0]], 0)
        act_g = jax.nn.silu(upper.astype(F32)).astype(BF16)
        moved = conv(act_g, weights, 1, width, False)
        await_state(2)
        x2 = (flat(state[m, 2]).astype(F32) - moved).astype(BF16)
        made[m, 2] = x2.reshape(rows, width, channels)
        send_edges(edge_b_copy, 0)
        send_on(m, 2)

        await_edges(edge_a_copy, 1)
        await_state(1)
        g2 = flat(state[m, 1])
        g2_wide = jnp.concatenate([edge_a[m, 0, 1], g2, edge_a[m, 1, 1]], 0)
        moved = conv(g2_wide, weights, 1, width, True) * silu_slope(y1.astype(F32))
        await_state(3)
        carried = (flat(state[m, 3]).astype(F32) + moved).astype(BF16)
        made[m, 3] = carried.reshape(rows, width, channels)
        send_edges(edge_b_copy, 1)
        send_on(m, 3)

        @pl.when(m == M - 1)
        def _():
            grads_g()
            send_pairs(groups // 2, groups - groups // 2)

        await_edges(edge_b_copy, 0)
        lower = jnp.concatenate([edge_b[m, 0, 0], x2, edge_b[m, 1, 0]], 0)
        act_f = jax.nn.silu(lower.astype(F32)).astype(BF16)
        x1 = (y1.astype(F32) - conv(act_f, weights, 0, width, False)).astype(BF16)
        made[m, 0] = x1.reshape(rows, width, channels)
        send_edges(edge_a_copy, 0, s > 0)
        send_on(m, 0)

        await_edges(edge_b_copy, 1)
        carried_wide = jnp.concatenate([edge_b[m, 0, 1], carried, edge_b[m, 1, 1]], 0)
        moved = conv(carried_wide, weights, 0, width, True) * silu_slope(x2.astype(F32))
        made[m, 1] = (g2.astype(F32) + moved).astype(BF16).reshape(rows, width, channels)
        send_edges(edge_a_copy, 1, s > 0)
        send_on(m, 1)

        @pl.when(m < M - 1)
        def _():
            grads_g()

        add_grads(acc, 0, act_f, carried, width)
        return carry

    lax.fori_loop(0, M, step, 0)
    send_pairs(0, groups // 2)
    send_sums(groups // 2, groups - groups // 2)
    send_sums(0, groups // 2)

    def deliver(source):
        out_streams[0, 0] = source[0]
        out_grads[0, 1] = source[1]
        out_streams[0, 1] = source[2]
        out_grads[0, 0] = source[3]

    @pl.when(s == 0)
    def _():
        deliver(made[M - 1])

    @pl.when(s > 0)
    def _():
        for i in range(4):
            result_copy(0, i).wait_recv()
        deliver(result[...])

    for side, row, there in sides:
        @pl.when(there)
        def _(side=side, row=row):
            for i in range(2):
                first_edge(i, side, row).wait_send()

    @pl.when(jnp.logical_not(last_sec))
    def _():
        for i in range(4):
            first_state(i).wait_send()

    def drain(m, carry):
        for side, row, there in sides:
            @pl.when(there)
            def _(side=side, row=row):
                for i in range(2):
                    edge_b_copy(m, i, side, row).wait_send()

            @pl.when(there & (s > 0))
            def _(side=side, row=row):
                for i in range(2):
                    edge_a_copy(m, i, side, row).wait_send()

        @pl.when(s > 0)
        def _():
            for i in range(4):
                state_copy(m, i).wait_send()

        @pl.when((s == 0) & (m < M - 1))
        def _():
            for i in range(4):
                result_copy(m, i).wait_send()
        return carry

    lax.fori_loop(0, M, drain, 0)

    def gather(i, carry):
        k = lax.rem(group + groups - i, groups)
        remote(
            sums.at[k], got.at[k], rs_send.at[k], rs_recv.at[k], s, 2 * k + half
        ).wait_recv()
        out_weights[0] += got[k].astype(F32)
        return carry

    lax.fori_loop(1, groups, gather, 0)
    out_weights[...] = out_weights[...] * scale

    def drain_terms(k, carry):
        pair_copy(k).wait_send()

        @pl.when(k != group)
        def _():
            sum_copy(k).wait_send()
        return carry

    lax.fori_loop(0, groups, drain_terms, 0)


def local(S, N, streams, cotangents, weights):
    mine, _, rows, width, channels = streams.shape
    layers = weights.shape[1]
    assert mine == 1 and layers == 1 and N % 2 == 0
    M = S
    scale = (M * rows * N * width) ** -0.5
    total = 18 * channels
    chunk = total // N
    sent = BF16 if chunk % 16 == 0 else F32
    dma = pltpu.SemaphoreType.DMA
    vmem = pl.BlockSpec(memory_space=pltpu.VMEM)
    shard = (rows, width, channels)
    edge = (2, 2, width, channels)
    return pl.pallas_call(
        functools.partial(body, S, N, scale),
        out_shape=(
            jax.ShapeDtypeStruct(streams.shape, BF16),
            jax.ShapeDtypeStruct(streams.shape, BF16),
            jax.ShapeDtypeStruct((1, chunk, channels), F32),
        ),
        in_specs=[pl.BlockSpec(memory_space=pl.ANY)] * 3,
        out_specs=(vmem,) * 3,
        scratch_shapes=[
            pltpu.VMEM(weights.shape[2:], BF16),
            pltpu.VMEM((4,) + shard, BF16),
            pltpu.VMEM((M, 4) + shard, BF16),
            pltpu.VMEM((M, 4) + shard, BF16),
            pltpu.VMEM((M,) + edge, BF16),
            pltpu.VMEM((M,) + edge, BF16),
            pltpu.VMEM((4,) + shard, BF16),
            pltpu.VMEM((total, channels), F32),
            pltpu.VMEM((N // 2, chunk, channels), sent),
            pltpu.VMEM((N // 2, chunk, channels), sent),
            pltpu.VMEM((N // 2, chunk, channels), sent),
            pltpu.VMEM((N // 2, chunk, channels), sent),
            dma((4,)), dma((2,)), dma((4,)), dma((2, 2)),
            dma((M, 4)), dma((M, 4)), dma((M, 4)), dma((M, 4)), dma((M, 4)), dma((M, 4)),
            dma((M, 4)), dma((4,)),
            dma((N // 2,)), dma((N // 2,)), dma((N // 2,)), dma((N // 2,)),
        ],
        compiler_params=pltpu.CompilerParams(
            collective_id=0, has_side_effects=True, vmem_limit_bytes=40 * 1024 * 1024
        ),
        cost_estimate=pl.CostEstimate(
            flops=M * 108 * rows * width * channels * channels,
            bytes_accessed=weights.size * 2,
            transcendentals=0,
        ),
    )(streams, cotangents, weights)


def solution(mesh):
    placed = (
        P("sec", None, "rows", None, None),
        P("sec", None, "rows", None, None),
        P("sec", None, None, None, None, None, None),
    )
    return jax.shard_map(
        functools.partial(local, mesh.shape["sec"], mesh.shape["rows"]),
        mesh=mesh,
        in_specs=placed,
        out_specs=(
            P("sec", None, "rows", None, None),
            P("sec", None, "rows", None, None),
            P("sec", "rows", None),
        ),
        check_vma=False,
    )
```

```python
import functools

import jax
import jax.numpy as jnp
from jax import lax
from jax.experimental import pallas as pl
from jax.experimental.pallas import tpu as pltpu
from jax.sharding import PartitionSpec as P

MESH = pl.DeviceIdType.MESH
F32 = jnp.float32
BF16 = jnp.bfloat16


def silu_slope(value):
    sig = jax.nn.sigmoid(value)
    return sig + value * sig * (1.0 - sig)


def shift_cols(value, by, width):
    pixels = value.shape[0]
    col = lax.rem(lax.broadcasted_iota(jnp.int32, value.shape, 0), width)
    rolled = pltpu.roll(value, by % pixels, axis=0)
    edge = 0 if by > 0 else width - 1
    return jnp.where(col == edge, 0.0, rolled)


def conv(field, kernel, width, turned):
    pixels, channels = field.shape[0] - 2 * width, field.shape[1]
    stacked = jnp.concatenate([field[a * width : a * width + pixels] for a in range(3)], 1)
    wide = lax.dot_general(
        stacked, kernel, (((1,), (1 if turned else 0,)), ((), ())), preferred_element_type=F32
    )
    left, centre, right = (wide[:, b * channels : (b + 1) * channels] for b in range(3))
    return centre + shift_cols(left, 1, width) + shift_cols(right, -1, width)


def add_grads(acc_ref, which, field, cotan, width):
    pixels, channels = cotan.shape
    wide = cotan.astype(F32)
    shifted = jnp.concatenate(
        [
            shift_cols(wide, -1, width).astype(BF16),
            cotan,
            shift_cols(wide, 1, width).astype(BF16),
        ],
        axis=1,
    )
    for a in range(3):
        term = lax.dot_general(
            field[a * width : a * width + pixels],
            shifted,
            (((0,), (0,)), ((), ())),
            preferred_element_type=F32,
        )
        for b in range(3):
            start = ((which * 3 + a) * 3 + b) * channels
            acc_ref[start : start + channels] += term[:, b * channels : (b + 1) * channels]


def body(
    S, N, scale,
    streams, cotangents, weights_in, out_streams, out_grads, out_weights,
    taps, turned, first, state, made, edge_a, edge_b, result, acc, terms, mid, sums, got,
    in_sem, w_sem, first_send, fedge_send, st_send, st_recv, ea_send, ea_recv, eb_send, eb_recv,
    res_send, res_recv, pair_send, pair_recv, rs_send, rs_recv,
):
    s, r = lax.axis_index("sec"), lax.axis_index("rows")
    M = S
    rows, width, channels = state.shape[2:]
    chunk = terms.shape[1]
    last_sec = s == S - 1
    below, above = lax.rem(r + 1, N), lax.rem(r + N - 1, N)
    has_above, has_below = r > 0, r < N - 1
    sides = ((0, above, has_above), (1, below, has_below))
    edge_row = (0, rows - 1)
    lower_sec = lax.rem(s + S - 1, S)
    half, group = lax.rem(r, 2), r // 2
    groups = N // 2
    partner = 2 * group + 1 - half

    def remote(src, dst, send, recv, sec, row):
        return pltpu.make_async_remote_copy(
            src_ref=src, dst_ref=dst, send_sem=send, recv_sem=recv,
            device_id=(sec, row), device_id_type=MESH,
        )

    own = S - 1 - s
    sources = (streams.at[0, 0], cotangents.at[0, 1], streams.at[0, 1], cotangents.at[0, 0])
    loads = [pltpu.make_async_copy(src, first.at[i], in_sem.at[i]) for i, src in enumerate(sources)]
    for load in loads:
        load.start()
    for which in (1, 0):
        for a in range(3):
            for b in range(3):
                rows_a, cols_b = pl.ds(a * channels, channels), pl.ds(b * channels, channels)
                pltpu.make_async_copy(
                    weights_in.at[0, 0, which, a, b], taps.at[which, rows_a, cols_b],
                    w_sem.at[0, which],
                ).start()
                pltpu.make_async_copy(
                    weights_in.at[0, 0, which, 2 - a, 2 - b], turned.at[which, cols_b, rows_a],
                    w_sem.at[1, which],
                ).start()

    barrier = pltpu.get_barrier_semaphore()
    for step in range(S):
        sec = lax.rem(s + step, S)
        if step > 0:
            pl.semaphore_signal(barrier, inc=1, device_id=(sec, r), device_id_type=MESH)
        for _, row, there in sides:
            if step > 0:
                @pl.when(there)
                def _(sec=sec, row=row):
                    pl.semaphore_signal(barrier, inc=1, device_id=(sec, row), device_id_type=MESH)
    for step in range(1, N):
        pl.semaphore_signal(
            barrier, inc=1, device_id=(s, lax.rem(r + step, N)), device_id_type=MESH
        )

    for side, _, there in sides:
        @pl.when(jnp.logical_not(there))
        def _(side=side):
            edge_a[:, side] = jnp.zeros(edge_a.shape[:1] + edge_a.shape[2:], BF16)
            edge_b[:, side] = jnp.zeros(edge_b.shape[:1] + edge_b.shape[2:], BF16)

    for load in loads:
        load.wait()

    @pl.when(last_sec)
    def _():
        state[0] = first[...]

    near = 1 + has_above.astype(jnp.int32) + has_below.astype(jnp.int32)
    pl.semaphore_wait(barrier, (S - 1) * near + N - 1)

    def first_edge(i, side, row):
        return remote(
            first.at[i, edge_row[side]], edge_a.at[own, 1 - side, i],
            fedge_send.at[side, i], ea_recv.at[own, 2 * (1 - side) + i], S - 1, row,
        )

    def first_state(i):
        return remote(
            first.at[i], state.at[own, i], first_send.at[i], st_recv.at[own, i], S - 1, r,
        )

    for i in range(2):
        for side, row, there in sides:
            @pl.when(there)
            def _(i=i, side=side, row=row):
                first_edge(i, side, row).start()

    @pl.when(jnp.logical_not(last_sec))
    def _():
        for i in range(4):
            first_state(i).start()

    acc[...] = jnp.zeros(acc.shape, F32)
    for i, kept in enumerate((taps, turned)):
        for which in range(2):
            pltpu.make_async_copy(kept.at[which], kept.at[which], w_sem.at[i, which]).wait()

    def state_copy(m, i):
        return remote(
            made.at[m, i], state.at[m, i], st_send.at[m, i], st_recv.at[m, i], lower_sec, r,
        )

    def result_copy(m, i):
        return remote(
            made.at[m, i], result.at[i], res_send.at[m, i], res_recv.at[i], S - 1 - m, r,
        )

    def edge_a_copy(m, i, side, row):
        return remote(
            made.at[m, i, edge_row[side]], edge_a.at[m, 1 - side, i],
            ea_send.at[m, 2 * side + i], ea_recv.at[m, 2 * (1 - side) + i], lower_sec, row,
        )

    def edge_b_copy(m, i, side, row):
        return remote(
            made.at[m, 2 + i, edge_row[side]], edge_b.at[m, 1 - side, i],
            eb_send.at[m, 2 * side + i], eb_recv.at[m, 2 * (1 - side) + i], s, row,
        )

    def send_on(m, i):
        @pl.when(s > 0)
        def _():
            state_copy(m, i).start()

        @pl.when((s == 0) & (m < M - 1))
        def _():
            result_copy(m, i).start()

    def rows_of(p):
        return pl.ds(pl.multiple_of(p * chunk, chunk), chunk)

    def pair_copy(k):
        return remote(terms.at[k], mid.at[k], pair_send.at[k], pair_recv.at[k], s, partner)

    def sum_copy(k):
        return remote(
            sums.at[k], got.at[group], rs_send.at[k], rs_recv.at[group], s, 2 * k + half
        )

    def send_pairs(low, count):
        def one(i, carry):
            k = low + lax.rem(group + 1 + i, count)
            terms[k] = acc[rows_of(2 * k + 1 - half)].astype(terms.dtype)
            pair_copy(k).start()
            return carry
        lax.fori_loop(0, count, one, 0)

    def send_sums(low, count):
        def one(i, carry):
            k = low + lax.rem(group + 1 + i, count)
            pair_copy(k).wait_recv()
            total = acc[rows_of(2 * k + half)] + mid[k].astype(F32)

            @pl.when(k == group)
            def _():
                out_weights[0] = total

            @pl.when(k != group)
            def _():
                sums[k] = total.astype(sums.dtype)
                sum_copy(k).start()
            return carry
        lax.fori_loop(0, count, one, 0)

    def flat(value):
        return value.reshape(-1, channels)

    def step(m, carry):
        arrives = jnp.logical_not(last_sec & (m == 0))

        def await_state(i):
            @pl.when(arrives)
            def _():
                state_copy(m, i).wait_recv()

        def await_edges(copy, i):
            for side, row, there in sides:
                @pl.when(there)
                def _(side=side, row=row):
                    copy(m, i, 1 - side, row).wait_recv()

        def send_edges(copy, i, ok=True):
            for side, row, there in sides:
                @pl.when(there & ok)
                def _(side=side, row=row):
                    copy(m, i, side, row).start()

        def grads_g():
            add_grads(acc, 1, act_g, g2, width)

        await_edges(edge_a_copy, 0)
        await_state(0)
        y1 = flat(state[m, 0])
        upper = jnp.concatenate([edge_a[m, 0, 0], y1, edge_a[m, 1, 0]], 0)
        act_g = jax.nn.silu(upper.astype(F32)).astype(BF16)
        moved = conv(act_g, taps[1], width, False)
        await_state(2)
        x2 = (flat(state[m, 2]).astype(F32) - moved).astype(BF16)
        made[m, 2] = x2.reshape(rows, width, channels)
        send_edges(edge_b_copy, 0)
        send_on(m, 2)

        await_edges(edge_a_copy, 1)
        await_state(1)
        g2 = flat(state[m, 1])
        g2_wide = jnp.concatenate([edge_a[m, 0, 1], g2, edge_a[m, 1, 1]], 0)
        moved = conv(g2_wide, turned[1], width, True) * silu_slope(y1.astype(F32))
        await_state(3)
        carried = (flat(state[m, 3]).astype(F32) + moved).astype(BF16)
        made[m, 3] = carried.reshape(rows, width, channels)
        send_edges(edge_b_copy, 1)
        send_on(m, 3)

        @pl.when(m == M - 1)
        def _():
            grads_g()
            send_pairs(groups // 2, groups - groups // 2)

        await_edges(edge_b_copy, 0)
        lower = jnp.concatenate([edge_b[m, 0, 0], x2, edge_b[m, 1, 0]], 0)
        act_f = jax.nn.silu(lower.astype(F32)).astype(BF16)
        x1 = (y1.astype(F32) - conv(act_f, taps[0], width, False)).astype(BF16)
        made[m, 0] = x1.reshape(rows, width, channels)
        send_edges(edge_a_copy, 0, s > 0)
        send_on(m, 0)

        await_edges(edge_b_copy, 1)
        carried_wide = jnp.concatenate([edge_b[m, 0, 1], carried, edge_b[m, 1, 1]], 0)
        moved = conv(carried_wide, turned[0], width, True) * silu_slope(x2.astype(F32))
        made[m, 1] = (g2.astype(F32) + moved).astype(BF16).reshape(rows, width, channels)
        send_edges(edge_a_copy, 1, s > 0)
        send_on(m, 1)

        @pl.when(m < M - 1)
        def _():
            grads_g()

        add_grads(acc, 0, act_f, carried, width)
        return carry

    lax.fori_loop(0, M, step, 0)
    send_pairs(0, groups // 2)
    send_sums(groups // 2, groups - groups // 2)
    send_sums(0, groups // 2)

    def deliver(source):
        out_streams[0, 0] = source[0]
        out_grads[0, 1] = source[1]
        out_streams[0, 1] = source[2]
        out_grads[0, 0] = source[3]

    @pl.when(s == 0)
    def _():
        deliver(made[M - 1])

    @pl.when(s > 0)
    def _():
        for i in range(4):
            result_copy(0, i).wait_recv()
        deliver(result[...])

    for side, row, there in sides:
        @pl.when(there)
        def _(side=side, row=row):
            for i in range(2):
                first_edge(i, side, row).wait_send()

    @pl.when(jnp.logical_not(last_sec))
    def _():
        for i in range(4):
            first_state(i).wait_send()

    def drain(m, carry):
        for side, row, there in sides:
            @pl.when(there)
            def _(side=side, row=row):
                for i in range(2):
                    edge_b_copy(m, i, side, row).wait_send()

            @pl.when(there & (s > 0))
            def _(side=side, row=row):
                for i in range(2):
                    edge_a_copy(m, i, side, row).wait_send()

        @pl.when(s > 0)
        def _():
            for i in range(4):
                state_copy(m, i).wait_send()

        @pl.when((s == 0) & (m < M - 1))
        def _():
            for i in range(4):
                result_copy(m, i).wait_send()
        return carry

    lax.fori_loop(0, M, drain, 0)

    def gather(i, carry):
        k = lax.rem(group + groups - i, groups)
        remote(
            sums.at[k], got.at[k], rs_send.at[k], rs_recv.at[k], s, 2 * k + half
        ).wait_recv()
        out_weights[0] += got[k].astype(F32)
        return carry

    lax.fori_loop(1, groups, gather, 0)
    out_weights[...] = out_weights[...] * scale

    def drain_terms(k, carry):
        pair_copy(k).wait_send()

        @pl.when(k != group)
        def _():
            sum_copy(k).wait_send()
        return carry

    lax.fori_loop(0, groups, drain_terms, 0)


def local(S, N, streams, cotangents, weights):
    mine, _, rows, width, channels = streams.shape
    layers = weights.shape[1]
    assert mine == 1 and layers == 1 and N % 2 == 0
    M = S
    scale = (M * rows * N * width) ** -0.5
    total = 18 * channels
    chunk = total // N
    sent = BF16 if chunk % 16 == 0 else F32
    dma = pltpu.SemaphoreType.DMA
    vmem = pl.BlockSpec(memory_space=pltpu.VMEM)
    shard = (rows, width, channels)
    edge = (2, 2, width, channels)
    return pl.pallas_call(
        functools.partial(body, S, N, scale),
        out_shape=(
            jax.ShapeDtypeStruct(streams.shape, BF16),
            jax.ShapeDtypeStruct(streams.shape, BF16),
            jax.ShapeDtypeStruct((1, chunk, channels), F32),
        ),
        in_specs=[pl.BlockSpec(memory_space=pltpu.HBM)] * 3,
        out_specs=(vmem,) * 3,
        scratch_shapes=[
            pltpu.VMEM((2, 3 * channels, 3 * channels), BF16),
            pltpu.VMEM((2, 3 * channels, 3 * channels), BF16),
            pltpu.VMEM((4,) + shard, BF16),
            pltpu.VMEM((M, 4) + shard, BF16),
            pltpu.VMEM((M, 4) + shard, BF16),
            pltpu.VMEM((M,) + edge, BF16),
            pltpu.VMEM((M,) + edge, BF16),
            pltpu.VMEM((4,) + shard, BF16),
            pltpu.VMEM((total, channels), F32),
            pltpu.VMEM((N // 2, chunk, channels), sent),
            pltpu.VMEM((N // 2, chunk, channels), sent),
            pltpu.VMEM((N // 2, chunk, channels), sent),
            pltpu.VMEM((N // 2, chunk, channels), sent),
            dma((4,)), dma((2, 2)), dma((4,)), dma((2, 2)),
            dma((M, 4)), dma((M, 4)), dma((M, 4)), dma((M, 4)), dma((M, 4)), dma((M, 4)),
            dma((M, 4)), dma((4,)),
            dma((N // 2,)), dma((N // 2,)), dma((N // 2,)), dma((N // 2,)),
        ],
        compiler_params=pltpu.CompilerParams(
            collective_id=0, has_side_effects=True, vmem_limit_bytes=64 * 1024 * 1024
        ),
        cost_estimate=pl.CostEstimate(
            flops=M * 108 * rows * width * channels * channels,
            bytes_accessed=weights.size * 2,
            transcendentals=0,
        ),
    )(streams, cotangents, weights)


def solution(mesh):
    placed = (
        P("sec", None, "rows", None, None),
        P("sec", None, "rows", None, None),
        P("sec", None, None, None, None, None, None),
    )
    return jax.shard_map(
        functools.partial(local, mesh.shape["sec"], mesh.shape["rows"]),
        mesh=mesh,
        in_specs=placed,
        out_specs=(
            P("sec", None, "rows", None, None),
            P("sec", None, "rows", None, None),
            P("sec", "rows", None),
        ),
        check_vma=False,
    )
```

```python
import functools

import jax
import jax.numpy as jnp
from jax import lax
from jax.experimental import pallas as pl
from jax.experimental.pallas import tpu as pltpu
from jax.sharding import PartitionSpec as P

MESH = pl.DeviceIdType.MESH
F32 = jnp.float32
BF16 = jnp.bfloat16


def silu_slope(value):
    sig = jax.nn.sigmoid(value)
    return sig + value * sig * (1.0 - sig)


def shift_cols(value, by, width):
    pixels = value.shape[0]
    col = lax.rem(lax.broadcasted_iota(jnp.int32, value.shape, 0), width)
    rolled = pltpu.roll(value, by % pixels, axis=0)
    edge = 0 if by > 0 else width - 1
    return jnp.where(col == edge, 0.0, rolled)


def conv(field, kernel, width):
    pixels, channels = field.shape[0] - 2 * width, field.shape[1]
    stacked = jnp.concatenate([field[a * width : a * width + pixels] for a in range(3)], 1)
    wide = jnp.dot(stacked, kernel, preferred_element_type=F32)
    left, centre, right = (wide[:, b * channels : (b + 1) * channels] for b in range(3))
    return centre + shift_cols(left, 1, width) + shift_cols(right, -1, width)


def all_grads(acc_ref, which, fields, cotans, width):
    pixels, channels = cotans[0].shape
    shifted = []
    for cotan in cotans:
        wide = cotan.astype(F32)
        shifted.append(
            jnp.concatenate(
                [
                    shift_cols(wide, -1, width).astype(BF16),
                    cotan,
                    shift_cols(wide, 1, width).astype(BF16),
                ],
                axis=1,
            )
        )
    shifted = jnp.concatenate(shifted, 0)
    for a in range(3):
        stacked = jnp.concatenate([f[a * width : a * width + pixels] for f in fields], 0)
        term = lax.dot_general(
            stacked, shifted, (((0,), (0,)), ((), ())), preferred_element_type=F32
        )
        for b in range(3):
            start = ((which * 3 + a) * 3 + b) * channels
            acc_ref[start : start + channels] = term[:, b * channels : (b + 1) * channels]


def body(
    S, N, scale,
    streams, cotangents, weights_in, out_streams, out_grads, out_weights,
    taps, turned, first, state, made, edge_a, edge_b, keep_g, keep_f, result, acc, terms, mid, sums, got,
    in_sem, w_sem, first_send, fedge_send, st_send, st_recv, ea_send, ea_recv, eb_send, eb_recv,
    res_send, res_recv, pair_send, pair_recv, rs_send, rs_recv, go,
):
    s, r = lax.axis_index("sec"), lax.axis_index("rows")
    M = S
    rows, width, channels = state.shape[2:]
    chunk = terms.shape[1]
    last_sec = s == S - 1
    below, above = lax.rem(r + 1, N), lax.rem(r + N - 1, N)
    has_above, has_below = r > 0, r < N - 1
    sides = ((0, above, has_above), (1, below, has_below))
    edge_row = (0, rows - 1)
    lower_sec = lax.rem(s + S - 1, S)
    half, group = lax.rem(r, 2), r // 2
    groups = N // 2
    partner = 2 * group + 1 - half

    def remote(src, dst, send, recv, sec, row):
        return pltpu.make_async_remote_copy(
            src_ref=src, dst_ref=dst, send_sem=send, recv_sem=recv,
            device_id=(sec, row), device_id_type=MESH,
        )

    own = S - 1 - s
    sources = (streams.at[0, 0], cotangents.at[0, 1], streams.at[0, 1], cotangents.at[0, 0])
    loads = [pltpu.make_async_copy(src, first.at[i], in_sem.at[i]) for i, src in enumerate(sources)]
    for load in loads:
        load.start()
    for which in (1, 0):
        for a in range(3):
            for b in range(3):
                rows_a, cols_b = pl.ds(a * channels, channels), pl.ds(b * channels, channels)
                pltpu.make_async_copy(
                    weights_in.at[0, 0, which, a, b], taps.at[which, rows_a, cols_b],
                    w_sem.at[which],
                ).start()

    barrier = pltpu.get_barrier_semaphore()
    for step in range(S):
        sec = lax.rem(s + step, S)
        if step > 0:
            pl.semaphore_signal(barrier, inc=1, device_id=(sec, r), device_id_type=MESH)
        for _, row, there in sides:
            if step > 0:
                @pl.when(there)
                def _(sec=sec, row=row):
                    pl.semaphore_signal(barrier, inc=1, device_id=(sec, row), device_id_type=MESH)
    for step in range(1, N):
        pl.semaphore_signal(
            barrier, inc=1, device_id=(s, lax.rem(r + step, N)), device_id_type=MESH
        )

    for side, _, there in sides:
        @pl.when(jnp.logical_not(there))
        def _(side=side):
            edge_a[:, side] = jnp.zeros(edge_a.shape[:1] + edge_a.shape[2:], BF16)
            edge_b[:, side] = jnp.zeros(edge_b.shape[:1] + edge_b.shape[2:], BF16)

    for load in loads:
        load.wait()

    @pl.when(last_sec)
    def _():
        state[0] = first[...]

    near = 1 + has_above.astype(jnp.int32) + has_below.astype(jnp.int32)
    pl.semaphore_wait(barrier, (S - 1) * near + N - 1)

    def first_edge(i, side, row):
        return remote(
            first.at[i, edge_row[side]], edge_a.at[own, 1 - side, i],
            fedge_send.at[side, i], ea_recv.at[own, 2 * (1 - side) + i], S - 1, row,
        )

    def first_state(i):
        return remote(
            first.at[i], state.at[own, i], first_send.at[i], st_recv.at[own, i], S - 1, r,
        )

    @pl.when(own >= 2)
    def _():
        pl.semaphore_wait(go, 1)

    for i in range(2):
        for side, row, there in sides:
            @pl.when(there)
            def _(i=i, side=side, row=row):
                first_edge(i, side, row).start()

    @pl.when(jnp.logical_not(last_sec))
    def _():
        for i in range(4):
            first_state(i).start()

    for which in (1, 0):
        pltpu.make_async_copy(taps.at[which], taps.at[which], w_sem.at[which]).wait()
        for a in range(3):
            for b in range(3):
                turned[which, a * channels : (a + 1) * channels, b * channels : (b + 1) * channels] = (
                    taps[
                        which,
                        (2 - a) * channels : (3 - a) * channels,
                        (2 - b) * channels : (3 - b) * channels,
                    ].T
                )

    def state_copy(m, i):
        return remote(
            made.at[m, i], state.at[m, i], st_send.at[m, i], st_recv.at[m, i], lower_sec, r,
        )

    def result_copy(m, i):
        return remote(
            made.at[m, i], result.at[i], res_send.at[m, i], res_recv.at[i], S - 1 - m, r,
        )

    def edge_a_copy(m, i, side, row):
        return remote(
            made.at[m, i, edge_row[side]], edge_a.at[m, 1 - side, i],
            ea_send.at[m, 2 * side + i], ea_recv.at[m, 2 * (1 - side) + i], lower_sec, row,
        )

    def edge_b_copy(m, i, side, row):
        return remote(
            made.at[m, 2 + i, edge_row[side]], edge_b.at[m, 1 - side, i],
            eb_send.at[m, 2 * side + i], eb_recv.at[m, 2 * (1 - side) + i], s, row,
        )

    def send_on(m, i):
        @pl.when(s > 0)
        def _():
            state_copy(m, i).start()

        @pl.when((s == 0) & (m < M - 1))
        def _():
            result_copy(m, i).start()

    def rows_of(p):
        return pl.ds(pl.multiple_of(p * chunk, chunk), chunk)

    def pair_copy(k):
        return remote(terms.at[k], mid.at[k], pair_send.at[k], pair_recv.at[k], s, partner)

    def sum_copy(k):
        return remote(
            sums.at[k], got.at[group], rs_send.at[k], rs_recv.at[group], s, 2 * k + half
        )

    def send_pairs(low, count):
        def one(i, carry):
            k = low + lax.rem(group + 1 + i, count)
            terms[k] = acc[rows_of(2 * k + 1 - half)].astype(terms.dtype)
            pair_copy(k).start()
            return carry
        lax.fori_loop(0, count, one, 0)

    def send_sums(low, count):
        def one(i, carry):
            k = low + lax.rem(group + 1 + i, count)
            pair_copy(k).wait_recv()
            total = acc[rows_of(2 * k + half)] + mid[k].astype(F32)

            @pl.when(k == group)
            def _():
                out_weights[0] = total

            @pl.when(k != group)
            def _():
                sums[k] = total.astype(sums.dtype)
                sum_copy(k).start()
            return carry
        lax.fori_loop(0, count, one, 0)

    def flat(value):
        return value.reshape(-1, channels)

    def step(m, carry):
        arrives = jnp.logical_not(last_sec & (m == 0))

        def await_state(i):
            @pl.when(arrives)
            def _():
                state_copy(m, i).wait_recv()

        def await_edges(copy, i):
            for side, row, there in sides:
                @pl.when(there)
                def _(side=side, row=row):
                    copy(m, i, 1 - side, row).wait_recv()

        def send_edges(copy, i, ok=True):
            for side, row, there in sides:
                @pl.when(there & ok)
                def _(side=side, row=row):
                    copy(m, i, side, row).start()

        def grads_f():
            crops = range(M)
            all_grads(acc, 0, [keep_f[c] for c in crops], [flat(made[c, 3]) for c in crops], width)
            send_pairs(0, groups // 2)

        last = m == M - 1

        await_edges(edge_a_copy, 0)
        await_state(0)
        y1 = flat(state[m, 0])
        upper = jnp.concatenate([edge_a[m, 0, 0], y1, edge_a[m, 1, 0]], 0)
        act_g = jax.nn.silu(upper.astype(F32)).astype(BF16)
        keep_g[m] = act_g
        moved = conv(act_g, taps[1], width)
        await_state(2)
        x2 = (flat(state[m, 2]).astype(F32) - moved).astype(BF16)
        made[m, 2] = x2.reshape(rows, width, channels)
        send_edges(edge_b_copy, 0)
        send_on(m, 2)

        @pl.when(last_sec & (m < M - 2))
        def _():
            pl.semaphore_signal(go, inc=1, device_id=(S - 3 - m, r), device_id_type=MESH)

        await_edges(edge_a_copy, 1)
        await_state(1)
        g2 = flat(state[m, 1])
        g2_wide = jnp.concatenate([edge_a[m, 0, 1], g2, edge_a[m, 1, 1]], 0)
        moved = conv(g2_wide, turned[1], width) * silu_slope(y1.astype(F32))
        await_state(3)
        carried = (flat(state[m, 3]).astype(F32) + moved).astype(BF16)
        made[m, 3] = carried.reshape(rows, width, channels)
        send_edges(edge_b_copy, 1)
        send_on(m, 3)

        @pl.when(last)
        def _():
            crops = range(M)
            all_grads(acc, 1, [keep_g[c] for c in crops], [flat(state[c, 1]) for c in crops], width)
            send_pairs(groups // 2, groups - groups // 2)

        await_edges(edge_b_copy, 0)
        lower = jnp.concatenate([edge_b[m, 0, 0], x2, edge_b[m, 1, 0]], 0)
        act_f = jax.nn.silu(lower.astype(F32)).astype(BF16)
        keep_f[m] = act_f

        @pl.when(last & (s == 0))
        def _():
            grads_f()

        x1 = (y1.astype(F32) - conv(act_f, taps[0], width)).astype(BF16)
        made[m, 0] = x1.reshape(rows, width, channels)
        send_edges(edge_a_copy, 0, s > 0)
        send_on(m, 0)

        await_edges(edge_b_copy, 1)
        carried_wide = jnp.concatenate([edge_b[m, 0, 1], carried, edge_b[m, 1, 1]], 0)
        moved = conv(carried_wide, turned[0], width) * silu_slope(x2.astype(F32))
        made[m, 1] = (g2.astype(F32) + moved).astype(BF16).reshape(rows, width, channels)
        send_edges(edge_a_copy, 1, s > 0)
        send_on(m, 1)

        @pl.when(last & (s > 0))
        def _():
            grads_f()

        return carry

    lax.fori_loop(0, M, step, 0)
    send_sums(groups // 2, groups - groups // 2)
    send_sums(0, groups // 2)

    def deliver(source):
        out_streams[0, 0] = source[0]
        out_grads[0, 1] = source[1]
        out_streams[0, 1] = source[2]
        out_grads[0, 0] = source[3]

    @pl.when(s == 0)
    def _():
        deliver(made[M - 1])

    @pl.when(s > 0)
    def _():
        for i in range(4):
            result_copy(0, i).wait_recv()
        deliver(result[...])

    for side, row, there in sides:
        @pl.when(there)
        def _(side=side, row=row):
            for i in range(2):
                first_edge(i, side, row).wait_send()

    @pl.when(jnp.logical_not(last_sec))
    def _():
        for i in range(4):
            first_state(i).wait_send()

    def drain(m, carry):
        for side, row, there in sides:
            @pl.when(there)
            def _(side=side, row=row):
                for i in range(2):
                    edge_b_copy(m, i, side, row).wait_send()

            @pl.when(there & (s > 0))
            def _(side=side, row=row):
                for i in range(2):
                    edge_a_copy(m, i, side, row).wait_send()

        @pl.when(s > 0)
        def _():
            for i in range(4):
                state_copy(m, i).wait_send()

        @pl.when((s == 0) & (m < M - 1))
        def _():
            for i in range(4):
                result_copy(m, i).wait_send()
        return carry

    lax.fori_loop(0, M, drain, 0)

    def gather(i, carry):
        k = lax.rem(group + groups - i, groups)
        remote(
            sums.at[k], got.at[k], rs_send.at[k], rs_recv.at[k], s, 2 * k + half
        ).wait_recv()
        out_weights[0] += got[k].astype(F32)
        return carry

    lax.fori_loop(1, groups, gather, 0)
    out_weights[...] = out_weights[...] * scale

    def drain_terms(k, carry):
        pair_copy(k).wait_send()

        @pl.when(k != group)
        def _():
            sum_copy(k).wait_send()
        return carry

    lax.fori_loop(0, groups, drain_terms, 0)


def local(S, N, streams, cotangents, weights):
    mine, _, rows, width, channels = streams.shape
    layers = weights.shape[1]
    assert mine == 1 and layers == 1 and N % 2 == 0
    M = S
    scale = (M * rows * N * width) ** -0.5
    total = 18 * channels
    chunk = total // N
    sent = BF16 if chunk % 16 == 0 else F32
    dma = pltpu.SemaphoreType.DMA
    vmem = pl.BlockSpec(memory_space=pltpu.VMEM)
    shard = (rows, width, channels)
    edge = (2, 2, width, channels)
    return pl.pallas_call(
        functools.partial(body, S, N, scale),
        out_shape=(
            jax.ShapeDtypeStruct(streams.shape, BF16),
            jax.ShapeDtypeStruct(streams.shape, BF16),
            jax.ShapeDtypeStruct((1, chunk, channels), F32),
        ),
        in_specs=[pl.BlockSpec(memory_space=pltpu.HBM)] * 3,
        out_specs=(vmem,) * 3,
        scratch_shapes=[
            pltpu.VMEM((2, 3 * channels, 3 * channels), BF16),
            pltpu.VMEM((2, 3 * channels, 3 * channels), BF16),
            pltpu.VMEM((4,) + shard, BF16),
            pltpu.VMEM((M, 4) + shard, BF16),
            pltpu.VMEM((M, 4) + shard, BF16),
            pltpu.VMEM((M,) + edge, BF16),
            pltpu.VMEM((M,) + edge, BF16),
            pltpu.VMEM((M, (rows + 2) * width, channels), BF16),
            pltpu.VMEM((M, (rows + 2) * width, channels), BF16),
            pltpu.VMEM((4,) + shard, BF16),
            pltpu.VMEM((total, channels), F32),
            pltpu.VMEM((N // 2, chunk, channels), sent),
            pltpu.VMEM((N // 2, chunk, channels), sent),
            pltpu.VMEM((N // 2, chunk, channels), sent),
            pltpu.VMEM((N // 2, chunk, channels), sent),
            dma((4,)), dma((2,)), dma((4,)), dma((2, 2)),
            dma((M, 4)), dma((M, 4)), dma((M, 4)), dma((M, 4)), dma((M, 4)), dma((M, 4)),
            dma((M, 4)), dma((4,)),
            dma((N // 2,)), dma((N // 2,)), dma((N // 2,)), dma((N // 2,)),
            pltpu.SemaphoreType.REGULAR,
        ],
        compiler_params=pltpu.CompilerParams(
            collective_id=0, has_side_effects=True, vmem_limit_bytes=251 * 256 * 1024
        ),
        cost_estimate=pl.CostEstimate(
            flops=M * 108 * rows * width * channels * channels,
            bytes_accessed=weights.size * 2,
            transcendentals=0,
        ),
    )(streams, cotangents, weights)


def solution(mesh):
    placed = (
        P("sec", None, "rows", None, None),
        P("sec", None, "rows", None, None),
        P("sec", None, None, None, None, None, None),
    )
    return jax.shard_map(
        functools.partial(local, mesh.shape["sec"], mesh.shape["rows"]),
        mesh=mesh,
        in_specs=placed,
        out_specs=(
            P("sec", None, "rows", None, None),
            P("sec", None, "rows", None, None),
            P("sec", "rows", None),
        ),
        check_vma=False,
    )
```

```python
import functools

import jax
import jax.numpy as jnp
from jax import lax
from jax.experimental import pallas as pl
from jax.experimental.pallas import tpu as pltpu
from jax.sharding import PartitionSpec as P

MESH = pl.DeviceIdType.MESH
F32 = jnp.float32
BF16 = jnp.bfloat16


def silu_slope(value):
    sig = jax.nn.sigmoid(value)
    return sig + value * sig * (1.0 - sig)


def shift_cols(value, by, width):
    pixels = value.shape[0]
    col = lax.rem(lax.broadcasted_iota(jnp.int32, value.shape, 0), width)
    rolled = pltpu.roll(value, by % pixels, axis=0)
    edge = 0 if by > 0 else width - 1
    return jnp.where(col == edge, 0.0, rolled)


def conv(field, kernel, width):
    pixels, channels = field.shape[0] - 2 * width, field.shape[1]
    stacked = jnp.concatenate([field[a * width : a * width + pixels] for a in range(3)], 1)
    wide = jnp.dot(stacked, kernel, preferred_element_type=F32)
    left, centre, right = (wide[:, b * channels : (b + 1) * channels] for b in range(3))
    return centre + shift_cols(left, 1, width) + shift_cols(right, -1, width)


def all_grads(acc_ref, which, fields, cotans, width):
    pixels, channels = cotans[0].shape
    shifted = []
    for cotan in cotans:
        wide = cotan.astype(F32)
        shifted.append(
            jnp.concatenate(
                [
                    shift_cols(wide, -1, width).astype(BF16),
                    cotan,
                    shift_cols(wide, 1, width).astype(BF16),
                ],
                axis=1,
            )
        )
    shifted = jnp.concatenate(shifted, 0)
    for a in range(3):
        stacked = jnp.concatenate([f[a * width : a * width + pixels] for f in fields], 0)
        term = lax.dot_general(
            stacked, shifted, (((0,), (0,)), ((), ())), preferred_element_type=F32
        )
        for b in range(3):
            start = ((which * 3 + a) * 3 + b) * channels
            acc_ref[start : start + channels] = term[:, b * channels : (b + 1) * channels]


def body(
    S, N, scale,
    streams, cotangents, weights_in, out_streams, out_grads, out_weights,
    taps, turned, first, state, made, edge_a, edge_b, keep_g, keep_f, result, acc, terms, mid, sums, got,
    in_sem, w_sem, first_send, fedge_send, st_send, st_recv, ea_send, ea_recv, eb_send, eb_recv,
    res_send, res_recv, pair_send, pair_recv, rs_send, rs_recv, go,
):
    s, r = lax.axis_index("sec"), lax.axis_index("rows")
    M = S
    rows, width, channels = state.shape[2:]
    chunk = terms.shape[1]
    last_sec = s == S - 1

    def placed(row):
        return 2 * (row // 2) + lax.rem(row + row // 2, 2)

    def sides_of(row):
        above, below = placed(lax.rem(row + N - 1, N)), placed(lax.rem(row + 1, N))
        return ((0, above, row > 0), (1, below, row < N - 1))

    block = placed(r)
    moved_block = block != r
    sides, first_sides = sides_of(block), sides_of(r)
    edge_row = (0, rows - 1)
    lower_sec = lax.rem(s + S - 1, S)
    half, group = lax.rem(r, 2), r // 2
    groups = N // 2
    partner = 2 * group + 1 - half

    def remote(src, dst, send, recv, sec, row):
        return pltpu.make_async_remote_copy(
            src_ref=src, dst_ref=dst, send_sem=send, recv_sem=recv,
            device_id=(sec, row), device_id_type=MESH,
        )

    own = S - 1 - s
    sources = (streams.at[0, 0], cotangents.at[0, 1], streams.at[0, 1], cotangents.at[0, 0])
    loads = [pltpu.make_async_copy(src, first.at[i], in_sem.at[i]) for i, src in enumerate(sources)]
    for load in loads:
        load.start()
    for which in (1, 0):
        for a in range(3):
            for b in range(3):
                rows_a, cols_b = pl.ds(a * channels, channels), pl.ds(b * channels, channels)
                pltpu.make_async_copy(
                    weights_in.at[0, 0, which, a, b], taps.at[which, rows_a, cols_b],
                    w_sem.at[which],
                ).start()

    barrier = pltpu.get_barrier_semaphore()
    pairs = ((group, True), (group - 1, group > 0), (group + 1, group < groups - 1))
    for step in range(1, N):
        pl.semaphore_signal(
            barrier, inc=1, device_id=(s, lax.rem(r + step, N)), device_id_type=MESH
        )
    for pair, there in pairs:
        @pl.when(there)
        def _(pair=pair):
            for step in range(1, S):
                for row in range(2):
                    pl.semaphore_signal(
                        barrier, inc=1, device_id=(lax.rem(s + step, S), 2 * pair + row),
                        device_id_type=MESH,
                    )

    for side, _, there in sides:
        @pl.when(jnp.logical_not(there))
        def _(side=side):
            edge_a[:, side] = jnp.zeros(edge_a.shape[:1] + edge_a.shape[2:], BF16)
            edge_b[:, side] = jnp.zeros(edge_b.shape[:1] + edge_b.shape[2:], BF16)

    for load in loads:
        load.wait()

    stays = last_sec & jnp.logical_not(moved_block)

    @pl.when(stays)
    def _():
        state[0] = first[...]

    def away(row):
        return jnp.logical_not(last_sec & (row == r))

    for side, row, there in first_sides:
        @pl.when(there & last_sec & (row == r))
        def _(side=side):
            for i in range(2):
                edge_a[0, 1 - side, i] = first[i, edge_row[side]]

    near = 1 + (group > 0).astype(jnp.int32) + (group < groups - 1).astype(jnp.int32)
    pl.semaphore_wait(barrier, 2 * (S - 1) * near + N - 1)

    def first_edge(i, side, row):
        return remote(
            first.at[i, edge_row[side]], edge_a.at[own, 1 - side, i],
            fedge_send.at[side, i], ea_recv.at[own, 2 * (1 - side) + i], S - 1, row,
        )

    def first_state(i):
        return remote(
            first.at[i], state.at[own, i], first_send.at[i], st_recv.at[own, i], S - 1, block,
        )

    @pl.when(own >= 2)
    def _():
        pl.semaphore_wait(go, 1)

    for i in range(2):
        for side, row, there in first_sides:
            @pl.when(there & away(row))
            def _(i=i, side=side, row=row):
                first_edge(i, side, row).start()

    @pl.when(jnp.logical_not(stays))
    def _():
        for i in range(4):
            first_state(i).start()

    for which in (1, 0):
        pltpu.make_async_copy(taps.at[which], taps.at[which], w_sem.at[which]).wait()
        for a in range(3):
            for b in range(3):
                turned[which, a * channels : (a + 1) * channels, b * channels : (b + 1) * channels] = (
                    taps[
                        which,
                        (2 - a) * channels : (3 - a) * channels,
                        (2 - b) * channels : (3 - b) * channels,
                    ].T
                )

    def state_copy(m, i):
        return remote(
            made.at[m, i], state.at[m, i], st_send.at[m, i], st_recv.at[m, i], lower_sec, r,
        )

    def result_copy(m, i):
        return remote(
            made.at[m, i], result.at[i], res_send.at[m, i], res_recv.at[i], S - 1 - m, block,
        )

    def edge_a_copy(m, i, side, row):
        return remote(
            made.at[m, i, edge_row[side]], edge_a.at[m, 1 - side, i],
            ea_send.at[m, 2 * side + i], ea_recv.at[m, 2 * (1 - side) + i], lower_sec, row,
        )

    def edge_b_copy(m, i, side, row):
        return remote(
            made.at[m, 2 + i, edge_row[side]], edge_b.at[m, 1 - side, i],
            eb_send.at[m, 2 * side + i], eb_recv.at[m, 2 * (1 - side) + i], s, row,
        )

    def send_on(m, i):
        @pl.when(s > 0)
        def _():
            state_copy(m, i).start()

        @pl.when((s == 0) & ((m < M - 1) | moved_block))
        def _():
            result_copy(m, i).start()

    def rows_of(p):
        return pl.ds(pl.multiple_of(p * chunk, chunk), chunk)

    def pair_copy(k):
        return remote(terms.at[k], mid.at[k], pair_send.at[k], pair_recv.at[k], s, partner)

    def sum_copy(k):
        return remote(
            sums.at[k], got.at[group], rs_send.at[k], rs_recv.at[group], s, 2 * k + half
        )

    def send_pairs(low, count):
        def one(i, carry):
            k = low + lax.rem(group + 1 + i, count)
            terms[k] = acc[rows_of(2 * k + 1 - half)].astype(terms.dtype)
            pair_copy(k).start()
            return carry
        lax.fori_loop(0, count, one, 0)

    def send_sums(low, count):
        def one(i, carry):
            k = low + lax.rem(group + 1 + i, count)
            pair_copy(k).wait_recv()
            total = acc[rows_of(2 * k + half)] + mid[k].astype(F32)

            @pl.when(k == group)
            def _():
                out_weights[0] = total

            @pl.when(k != group)
            def _():
                sums[k] = total.astype(sums.dtype)
                sum_copy(k).start()
            return carry
        lax.fori_loop(0, count, one, 0)

    def flat(value):
        return value.reshape(-1, channels)

    def step(m, carry):
        arrives = jnp.logical_not(stays & (m == 0))

        def await_state(i):
            @pl.when(arrives)
            def _():
                state_copy(m, i).wait_recv()

        def await_edges(copy, i):
            for side, row, there in sides:
                if copy is edge_a_copy:
                    here = last_sec & (m == 0) & (block + 2 * side - 1 == r)
                    there = there & jnp.logical_not(here)

                @pl.when(there)
                def _(side=side, row=row):
                    copy(m, i, 1 - side, row).wait_recv()

        def send_edges(copy, i, ok=True):
            for side, row, there in sides:
                @pl.when(there & ok)
                def _(side=side, row=row):
                    copy(m, i, side, row).start()

        def grads_f():
            crops = range(M)
            all_grads(acc, 0, [keep_f[c] for c in crops], [flat(made[c, 3]) for c in crops], width)
            send_pairs(0, groups // 2)

        last = m == M - 1

        await_edges(edge_a_copy, 0)
        await_state(0)
        y1 = flat(state[m, 0])
        upper = jnp.concatenate([edge_a[m, 0, 0], y1, edge_a[m, 1, 0]], 0)
        act_g = jax.nn.silu(upper.astype(F32)).astype(BF16)
        keep_g[m] = act_g
        moved = conv(act_g, taps[1], width)
        await_state(2)
        x2 = (flat(state[m, 2]).astype(F32) - moved).astype(BF16)
        made[m, 2] = x2.reshape(rows, width, channels)
        send_edges(edge_b_copy, 0)
        send_on(m, 2)

        @pl.when(last_sec & (m < M - 2))
        def _():
            pl.semaphore_signal(go, inc=1, device_id=(S - 3 - m, block), device_id_type=MESH)

        await_edges(edge_a_copy, 1)
        await_state(1)
        g2 = flat(state[m, 1])
        g2_wide = jnp.concatenate([edge_a[m, 0, 1], g2, edge_a[m, 1, 1]], 0)
        moved = conv(g2_wide, turned[1], width) * silu_slope(y1.astype(F32))
        await_state(3)
        carried = (flat(state[m, 3]).astype(F32) + moved).astype(BF16)
        made[m, 3] = carried.reshape(rows, width, channels)
        send_edges(edge_b_copy, 1)
        send_on(m, 3)

        @pl.when(last)
        def _():
            crops = range(M)
            all_grads(acc, 1, [keep_g[c] for c in crops], [flat(state[c, 1]) for c in crops], width)
            send_pairs(groups // 2, groups - groups // 2)

        await_edges(edge_b_copy, 0)
        lower = jnp.concatenate([edge_b[m, 0, 0], x2, edge_b[m, 1, 0]], 0)
        act_f = jax.nn.silu(lower.astype(F32)).astype(BF16)
        keep_f[m] = act_f

        @pl.when(last & (s == 0))
        def _():
            grads_f()

        x1 = (y1.astype(F32) - conv(act_f, taps[0], width)).astype(BF16)
        made[m, 0] = x1.reshape(rows, width, channels)
        send_edges(edge_a_copy, 0, s > 0)
        send_on(m, 0)

        await_edges(edge_b_copy, 1)
        carried_wide = jnp.concatenate([edge_b[m, 0, 1], carried, edge_b[m, 1, 1]], 0)
        moved = conv(carried_wide, turned[0], width) * silu_slope(x2.astype(F32))
        made[m, 1] = (g2.astype(F32) + moved).astype(BF16).reshape(rows, width, channels)
        send_edges(edge_a_copy, 1, s > 0)
        send_on(m, 1)

        @pl.when(last & (s > 0))
        def _():
            grads_f()

        return carry

    lax.fori_loop(0, M, step, 0)
    send_sums(groups // 2, groups - groups // 2)
    send_sums(0, groups // 2)

    def deliver(source):
        out_streams[0, 0] = source[0]
        out_grads[0, 1] = source[1]
        out_streams[0, 1] = source[2]
        out_grads[0, 0] = source[3]

    @pl.when((s == 0) & jnp.logical_not(moved_block))
    def _():
        deliver(made[M - 1])

    @pl.when((s > 0) | moved_block)
    def _():
        for i in range(4):
            result_copy(0, i).wait_recv()
        deliver(result[...])

    for side, row, there in first_sides:
        @pl.when(there & away(row))
        def _(side=side, row=row):
            for i in range(2):
                first_edge(i, side, row).wait_send()

    @pl.when(jnp.logical_not(stays))
    def _():
        for i in range(4):
            first_state(i).wait_send()

    def drain(m, carry):
        for side, row, there in sides:
            @pl.when(there)
            def _(side=side, row=row):
                for i in range(2):
                    edge_b_copy(m, i, side, row).wait_send()

            @pl.when(there & (s > 0))
            def _(side=side, row=row):
                for i in range(2):
                    edge_a_copy(m, i, side, row).wait_send()

        @pl.when(s > 0)
        def _():
            for i in range(4):
                state_copy(m, i).wait_send()

        @pl.when((s == 0) & ((m < M - 1) | moved_block))
        def _():
            for i in range(4):
                result_copy(m, i).wait_send()
        return carry

    lax.fori_loop(0, M, drain, 0)

    def gather(i, carry):
        k = lax.rem(group + groups - i, groups)
        remote(
            sums.at[k], got.at[k], rs_send.at[k], rs_recv.at[k], s, 2 * k + half
        ).wait_recv()
        out_weights[0] += got[k].astype(F32)
        return carry

    lax.fori_loop(1, groups, gather, 0)
    out_weights[...] = out_weights[...] * scale

    def drain_terms(k, carry):
        pair_copy(k).wait_send()

        @pl.when(k != group)
        def _():
            sum_copy(k).wait_send()
        return carry

    lax.fori_loop(0, groups, drain_terms, 0)


def local(S, N, streams, cotangents, weights):
    mine, _, rows, width, channels = streams.shape
    layers = weights.shape[1]
    assert mine == 1 and layers == 1 and N % 2 == 0
    M = S
    scale = (M * rows * N * width) ** -0.5
    total = 18 * channels
    chunk = total // N
    sent = BF16 if chunk % 16 == 0 else F32
    dma = pltpu.SemaphoreType.DMA
    vmem = pl.BlockSpec(memory_space=pltpu.VMEM)
    shard = (rows, width, channels)
    edge = (2, 2, width, channels)
    return pl.pallas_call(
        functools.partial(body, S, N, scale),
        out_shape=(
            jax.ShapeDtypeStruct(streams.shape, BF16),
            jax.ShapeDtypeStruct(streams.shape, BF16),
            jax.ShapeDtypeStruct((1, chunk, channels), F32),
        ),
        in_specs=[pl.BlockSpec(memory_space=pltpu.HBM)] * 3,
        out_specs=(vmem,) * 3,
        scratch_shapes=[
            pltpu.VMEM((2, 3 * channels, 3 * channels), BF16),
            pltpu.VMEM((2, 3 * channels, 3 * channels), BF16),
            pltpu.VMEM((4,) + shard, BF16),
            pltpu.VMEM((M, 4) + shard, BF16),
            pltpu.VMEM((M, 4) + shard, BF16),
            pltpu.VMEM((M,) + edge, BF16),
            pltpu.VMEM((M,) + edge, BF16),
            pltpu.VMEM((M, (rows + 2) * width, channels), BF16),
            pltpu.VMEM((M, (rows + 2) * width, channels), BF16),
            pltpu.VMEM((4,) + shard, BF16),
            pltpu.VMEM((total, channels), F32),
            pltpu.VMEM((N // 2, chunk, channels), sent),
            pltpu.VMEM((N // 2, chunk, channels), sent),
            pltpu.VMEM((N // 2, chunk, channels), sent),
            pltpu.VMEM((N // 2, chunk, channels), sent),
            dma((4,)), dma((2,)), dma((4,)), dma((2, 2)),
            dma((M, 4)), dma((M, 4)), dma((M, 4)), dma((M, 4)), dma((M, 4)), dma((M, 4)),
            dma((M, 4)), dma((4,)),
            dma((N // 2,)), dma((N // 2,)), dma((N // 2,)), dma((N // 2,)),
            pltpu.SemaphoreType.REGULAR,
        ],
        compiler_params=pltpu.CompilerParams(
            collective_id=0, has_side_effects=True, vmem_limit_bytes=251 * 256 * 1024
        ),
        cost_estimate=pl.CostEstimate(
            flops=M * 108 * rows * width * channels * channels,
            bytes_accessed=weights.size * 2,
            transcendentals=0,
        ),
    )(streams, cotangents, weights)


def solution(mesh):
    placed = (
        P("sec", None, "rows", None, None),
        P("sec", None, "rows", None, None),
        P("sec", None, None, None, None, None, None),
    )
    return jax.shard_map(
        functools.partial(local, mesh.shape["sec"], mesh.shape["rows"]),
        mesh=mesh,
        in_specs=placed,
        out_specs=(
            P("sec", None, "rows", None, None),
            P("sec", None, "rows", None, None),
            P("sec", "rows", None),
        ),
        check_vma=False,
    )
```

```python
import functools

import jax
import jax.numpy as jnp
from jax import lax
from jax.experimental import pallas as pl
from jax.experimental.pallas import tpu as pltpu
from jax.sharding import PartitionSpec as P

MESH = pl.DeviceIdType.MESH
F32 = jnp.float32
BF16 = jnp.bfloat16


def sigmoid(value):
    return 0.5 * jnp.tanh(0.5 * value) + 0.5


def silu_slope(value, sig):
    return sig + value * sig * (1.0 - sig)


def shift_cols(value, by, width):
    shaped = value.reshape(-1, width, value.shape[1])
    rolled = pltpu.roll(shaped, by % width, axis=1)
    col = lax.broadcasted_iota(jnp.int32, shaped.shape, 1)
    edge = 0 if by > 0 else width - 1
    return jnp.where(col == edge, 0.0, rolled).reshape(value.shape)


def conv(field, kernel, width):
    pixels, channels = field.shape[0] - 2 * width, field.shape[1]
    stacked = jnp.concatenate([field[a * width : a * width + pixels] for a in range(3)], 1)
    wide = jnp.dot(stacked, kernel, preferred_element_type=F32)
    left, centre, right = (wide[:, b * channels : (b + 1) * channels] for b in range(3))
    return centre + shift_cols(left, 1, width) + shift_cols(right, -1, width)


def all_grads(acc_ref, which, fields, cotans, width):
    pixels, channels = cotans[0].shape
    shifted = []
    for cotan in cotans:
        wide = cotan.astype(F32)
        shifted.append(
            jnp.concatenate(
                [
                    shift_cols(wide, -1, width).astype(BF16),
                    cotan,
                    shift_cols(wide, 1, width).astype(BF16),
                ],
                axis=1,
            )
        )
    shifted = jnp.concatenate(shifted, 0)
    for a in range(3):
        stacked = jnp.concatenate([f[a * width : a * width + pixels] for f in fields], 0)
        term = lax.dot_general(
            stacked, shifted, (((0,), (0,)), ((), ())), preferred_element_type=F32
        )
        for b in range(3):
            start = ((which * 3 + a) * 3 + b) * channels
            acc_ref[start : start + channels] = term[:, b * channels : (b + 1) * channels]


def body(
    S, N, scale,
    streams, cotangents, weights_in, out_streams, out_grads, out_weights,
    taps, turned, first, state, made, edge_a, edge_b, keep_g, keep_f, result, acc, terms, mid, sums, got,
    in_sem, w_sem, first_send, fedge_send, st_send, st_recv, ea_send, ea_recv, eb_send, eb_recv,
    res_send, res_recv, pair_send, pair_recv, rs_send, rs_recv, go,
):
    s, r = lax.axis_index("sec"), lax.axis_index("rows")
    M = S
    rows, width, channels = state.shape[2:]
    chunk = terms.shape[1]
    last_sec = s == S - 1

    def placed(row):
        return 2 * (row // 2) + lax.rem(row + row // 2, 2)

    def sides_of(row):
        above, below = placed(lax.rem(row + N - 1, N)), placed(lax.rem(row + 1, N))
        return ((0, above, row > 0), (1, below, row < N - 1))

    block = placed(r)
    moved_block = block != r
    sides, first_sides = sides_of(block), sides_of(r)
    edge_row = (0, rows - 1)
    lower_sec = lax.rem(s + S - 1, S)
    half, group = lax.rem(r, 2), r // 2
    groups = N // 2
    partner = 2 * group + 1 - half

    def remote(src, dst, send, recv, sec, row):
        return pltpu.make_async_remote_copy(
            src_ref=src, dst_ref=dst, send_sem=send, recv_sem=recv,
            device_id=(sec, row), device_id_type=MESH,
        )

    own = S - 1 - s
    sources = (streams.at[0, 0], cotangents.at[0, 1], streams.at[0, 1], cotangents.at[0, 0])
    loads = [pltpu.make_async_copy(src, first.at[i], in_sem.at[i]) for i, src in enumerate(sources)]
    for load in loads:
        load.start()
    for which in (1, 0):
        for a in range(3):
            for b in range(3):
                rows_a, cols_b = pl.ds(a * channels, channels), pl.ds(b * channels, channels)
                pltpu.make_async_copy(
                    weights_in.at[0, 0, which, a, b], taps.at[which, rows_a, cols_b],
                    w_sem.at[which],
                ).start()

    barrier = pltpu.get_barrier_semaphore()
    pairs = ((group, True), (group - 1, group > 0), (group + 1, group < groups - 1))
    for step in range(1, N):
        pl.semaphore_signal(
            barrier, inc=1, device_id=(s, lax.rem(r + step, N)), device_id_type=MESH
        )
    for pair, there in pairs:
        @pl.when(there)
        def _(pair=pair):
            for step in range(1, S):
                for row in range(2):
                    pl.semaphore_signal(
                        barrier, inc=1, device_id=(lax.rem(s + step, S), 2 * pair + row),
                        device_id_type=MESH,
                    )

    for side, _, there in sides:
        @pl.when(jnp.logical_not(there))
        def _(side=side):
            edge_a[:, side] = jnp.zeros(edge_a.shape[:1] + edge_a.shape[2:], BF16)
            edge_b[:, side] = jnp.zeros(edge_b.shape[:1] + edge_b.shape[2:], BF16)

    for load in loads:
        load.wait()

    stays = last_sec & jnp.logical_not(moved_block)

    @pl.when(stays)
    def _():
        state[0] = first[...]

    def away(row):
        return jnp.logical_not(last_sec & (row == r))

    for side, row, there in first_sides:
        @pl.when(there & last_sec & (row == r))
        def _(side=side):
            for i in range(2):
                edge_a[0, 1 - side, i] = first[i, edge_row[side]]

    near = 1 + (group > 0).astype(jnp.int32) + (group < groups - 1).astype(jnp.int32)
    pl.semaphore_wait(barrier, 2 * (S - 1) * near + N - 1)

    def first_edge(i, side, row):
        return remote(
            first.at[i, edge_row[side]], edge_a.at[own, 1 - side, i],
            fedge_send.at[side, i], ea_recv.at[own, 2 * (1 - side) + i], S - 1, row,
        )

    def first_state(i):
        return remote(
            first.at[i], state.at[own, i], first_send.at[i], st_recv.at[own, i], S - 1, block,
        )

    @pl.when(own >= 2)
    def _():
        pl.semaphore_wait(go, 1)

    for i in range(2):
        for side, row, there in first_sides:
            @pl.when(there & away(row))
            def _(i=i, side=side, row=row):
                first_edge(i, side, row).start()

    @pl.when(jnp.logical_not(stays))
    def _():
        for i in range(4):
            first_state(i).start()

    for which in (1, 0):
        pltpu.make_async_copy(taps.at[which], taps.at[which], w_sem.at[which]).wait()
        for a in range(3):
            for b in range(3):
                turned[which, a * channels : (a + 1) * channels, b * channels : (b + 1) * channels] = (
                    taps[
                        which,
                        (2 - a) * channels : (3 - a) * channels,
                        (2 - b) * channels : (3 - b) * channels,
                    ].T
                )

    def state_copy(m, i):
        return remote(
            made.at[m, i], state.at[m, i], st_send.at[m, i], st_recv.at[m, i], lower_sec, r,
        )

    def result_copy(m, i):
        return remote(
            made.at[m, i], result.at[i], res_send.at[m, i], res_recv.at[i], S - 1 - m, block,
        )

    def edge_a_copy(m, i, side, row):
        return remote(
            made.at[m, i, edge_row[side]], edge_a.at[m, 1 - side, i],
            ea_send.at[m, 2 * side + i], ea_recv.at[m, 2 * (1 - side) + i], lower_sec, row,
        )

    def edge_b_copy(m, i, side, row):
        return remote(
            made.at[m, 2 + i, edge_row[side]], edge_b.at[m, 1 - side, i],
            eb_send.at[m, 2 * side + i], eb_recv.at[m, 2 * (1 - side) + i], s, row,
        )

    def send_on(m, i):
        @pl.when(s > 0)
        def _():
            state_copy(m, i).start()

        @pl.when((s == 0) & ((m < M - 1) | moved_block))
        def _():
            result_copy(m, i).start()

    def rows_of(p):
        return pl.ds(pl.multiple_of(p * chunk, chunk), chunk)

    def pair_copy(k):
        return remote(terms.at[k], mid.at[k], pair_send.at[k], pair_recv.at[k], s, partner)

    def sum_copy(k):
        return remote(
            sums.at[k], got.at[group], rs_send.at[k], rs_recv.at[group], s, 2 * k + half
        )

    def send_pairs(low, count):
        def one(i, carry):
            k = low + lax.rem(group + 1 + i, count)
            terms[k] = acc[rows_of(2 * k + 1 - half)].astype(terms.dtype)
            pair_copy(k).start()
            return carry
        lax.fori_loop(0, count, one, 0)

    def send_sums(low, count):
        def one(i, carry):
            k = low + lax.rem(group + 1 + i, count)
            pair_copy(k).wait_recv()
            total = acc[rows_of(2 * k + half)] + mid[k].astype(F32)

            @pl.when(k == group)
            def _():
                out_weights[0] = total

            @pl.when(k != group)
            def _():
                sums[k] = total.astype(sums.dtype)
                sum_copy(k).start()
            return carry
        lax.fori_loop(0, count, one, 0)

    def flat(value):
        return value.reshape(-1, channels)

    def step(m, carry):
        arrives = jnp.logical_not(stays & (m == 0))

        def await_state(i):
            @pl.when(arrives)
            def _():
                state_copy(m, i).wait_recv()

        def await_edges(copy, i):
            for side, row, there in sides:
                if copy is edge_a_copy:
                    here = last_sec & (m == 0) & (block + 2 * side - 1 == r)
                    there = there & jnp.logical_not(here)

                @pl.when(there)
                def _(side=side, row=row):
                    copy(m, i, 1 - side, row).wait_recv()

        def send_edges(copy, i, ok=True):
            for side, row, there in sides:
                @pl.when(there & ok)
                def _(side=side, row=row):
                    copy(m, i, side, row).start()

        def grads_g():
            crops = range(M)
            all_grads(acc, 1, [keep_g[c] for c in crops], [flat(state[c, 1]) for c in crops], width)
            send_pairs(groups // 2, groups - groups // 2)

        def grads_f():
            crops = range(M)
            all_grads(acc, 0, [keep_f[c] for c in crops], [flat(made[c, 3]) for c in crops], width)
            send_pairs(0, groups // 2)

        last = m == M - 1

        await_edges(edge_a_copy, 0)
        await_state(0)
        y1 = flat(state[m, 0])
        upper = jnp.concatenate([edge_a[m, 0, 0], y1, edge_a[m, 1, 0]], 0)
        upper = upper.astype(F32)
        sig = sigmoid(upper)
        act_g = (upper * sig).astype(BF16)
        slope = silu_slope(upper[width:-width], sig[width:-width])
        keep_g[m] = act_g
        moved = conv(act_g, taps[1], width)
        await_state(2)
        x2 = (flat(state[m, 2]).astype(F32) - moved).astype(BF16)
        made[m, 2] = x2.reshape(rows, width, channels)
        send_edges(edge_b_copy, 0)
        send_on(m, 2)

        @pl.when(last_sec & (m < M - 2))
        def _():
            pl.semaphore_signal(go, inc=1, device_id=(S - 3 - m, block), device_id_type=MESH)

        await_edges(edge_a_copy, 1)
        await_state(1)
        g2 = flat(state[m, 1])
        g2_wide = jnp.concatenate([edge_a[m, 0, 1], g2, edge_a[m, 1, 1]], 0)
        moved = conv(g2_wide, turned[1], width) * slope
        await_state(3)
        carried = (flat(state[m, 3]).astype(F32) + moved).astype(BF16)
        made[m, 3] = carried.reshape(rows, width, channels)
        send_edges(edge_b_copy, 1)
        send_on(m, 3)

        @pl.when(last & (s == 0))
        def _():
            grads_g()

        await_edges(edge_b_copy, 0)
        lower = jnp.concatenate([edge_b[m, 0, 0], x2, edge_b[m, 1, 0]], 0)
        lower = lower.astype(F32)
        sig = sigmoid(lower)
        act_f = (lower * sig).astype(BF16)
        slope = silu_slope(lower[width:-width], sig[width:-width])
        keep_f[m] = act_f

        @pl.when(last & (s == 0))
        def _():
            grads_f()

        x1 = (y1.astype(F32) - conv(act_f, taps[0], width)).astype(BF16)
        made[m, 0] = x1.reshape(rows, width, channels)
        send_edges(edge_a_copy, 0, s > 0)
        send_on(m, 0)

        await_edges(edge_b_copy, 1)
        carried_wide = jnp.concatenate([edge_b[m, 0, 1], carried, edge_b[m, 1, 1]], 0)
        moved = conv(carried_wide, turned[0], width) * slope
        made[m, 1] = (g2.astype(F32) + moved).astype(BF16).reshape(rows, width, channels)
        send_edges(edge_a_copy, 1, s > 0)
        send_on(m, 1)

        @pl.when(last & (s > 0))
        def _():
            grads_g()
            grads_f()

        return carry

    lax.fori_loop(0, M, step, 0)
    send_sums(groups // 2, groups - groups // 2)
    send_sums(0, groups // 2)

    def deliver(source):
        out_streams[0, 0] = source[0]
        out_grads[0, 1] = source[1]
        out_streams[0, 1] = source[2]
        out_grads[0, 0] = source[3]

    @pl.when((s == 0) & jnp.logical_not(moved_block))
    def _():
        deliver(made[M - 1])

    @pl.when((s > 0) | moved_block)
    def _():
        for i in range(4):
            result_copy(0, i).wait_recv()
        deliver(result[...])

    for side, row, there in first_sides:
        @pl.when(there & away(row))
        def _(side=side, row=row):
            for i in range(2):
                first_edge(i, side, row).wait_send()

    @pl.when(jnp.logical_not(stays))
    def _():
        for i in range(4):
            first_state(i).wait_send()

    def drain(m, carry):
        for side, row, there in sides:
            @pl.when(there)
            def _(side=side, row=row):
                for i in range(2):
                    edge_b_copy(m, i, side, row).wait_send()

            @pl.when(there & (s > 0))
            def _(side=side, row=row):
                for i in range(2):
                    edge_a_copy(m, i, side, row).wait_send()

        @pl.when(s > 0)
        def _():
            for i in range(4):
                state_copy(m, i).wait_send()

        @pl.when((s == 0) & ((m < M - 1) | moved_block))
        def _():
            for i in range(4):
                result_copy(m, i).wait_send()
        return carry

    lax.fori_loop(0, M, drain, 0)

    def gather(i, carry):
        k = lax.rem(group + groups - i, groups)
        remote(
            sums.at[k], got.at[k], rs_send.at[k], rs_recv.at[k], s, 2 * k + half
        ).wait_recv()
        out_weights[0] += got[k].astype(F32)
        return carry

    lax.fori_loop(1, groups, gather, 0)
    out_weights[...] = out_weights[...] * scale

    def drain_terms(k, carry):
        pair_copy(k).wait_send()

        @pl.when(k != group)
        def _():
            sum_copy(k).wait_send()
        return carry

    lax.fori_loop(0, groups, drain_terms, 0)


def local(S, N, streams, cotangents, weights):
    mine, _, rows, width, channels = streams.shape
    layers = weights.shape[1]
    assert mine == 1 and layers == 1 and N % 2 == 0
    M = S
    scale = (M * rows * N * width) ** -0.5
    total = 18 * channels
    chunk = total // N
    sent = BF16 if chunk % 16 == 0 else F32
    dma = pltpu.SemaphoreType.DMA
    vmem = pl.BlockSpec(memory_space=pltpu.VMEM)
    shard = (rows, width, channels)
    edge = (2, 2, width, channels)
    return pl.pallas_call(
        functools.partial(body, S, N, scale),
        out_shape=(
            jax.ShapeDtypeStruct(streams.shape, BF16),
            jax.ShapeDtypeStruct(streams.shape, BF16),
            jax.ShapeDtypeStruct((1, chunk, channels), F32),
        ),
        in_specs=[pl.BlockSpec(memory_space=pltpu.HBM)] * 3,
        out_specs=(vmem,) * 3,
        scratch_shapes=[
            pltpu.VMEM((2, 3 * channels, 3 * channels), BF16),
            pltpu.VMEM((2, 3 * channels, 3 * channels), BF16),
            pltpu.VMEM((4,) + shard, BF16),
            pltpu.VMEM((M, 4) + shard, BF16),
            pltpu.VMEM((M, 4) + shard, BF16),
            pltpu.VMEM((M,) + edge, BF16),
            pltpu.VMEM((M,) + edge, BF16),
            pltpu.VMEM((M, (rows + 2) * width, channels), BF16),
            pltpu.VMEM((M, (rows + 2) * width, channels), BF16),
            pltpu.VMEM((4,) + shard, BF16),
            pltpu.VMEM((total, channels), F32),
            pltpu.VMEM((N // 2, chunk, channels), sent),
            pltpu.VMEM((N // 2, chunk, channels), sent),
            pltpu.VMEM((N // 2, chunk, channels), sent),
            pltpu.VMEM((N // 2, chunk, channels), sent),
            dma((4,)), dma((2,)), dma((4,)), dma((2, 2)),
            dma((M, 4)), dma((M, 4)), dma((M, 4)), dma((M, 4)), dma((M, 4)), dma((M, 4)),
            dma((M, 4)), dma((4,)),
            dma((N // 2,)), dma((N // 2,)), dma((N // 2,)), dma((N // 2,)),
            pltpu.SemaphoreType.REGULAR,
        ],
        compiler_params=pltpu.CompilerParams(
            collective_id=0, has_side_effects=True, vmem_limit_bytes=52 * 1024 * 1024
        ),
        cost_estimate=pl.CostEstimate(
            flops=M * 108 * rows * width * channels * channels,
            bytes_accessed=weights.size * 2,
            transcendentals=0,
        ),
    )(streams, cotangents, weights)


def solution(mesh):
    placed = (
        P("sec", None, "rows", None, None),
        P("sec", None, "rows", None, None),
        P("sec", None, None, None, None, None, None),
    )
    return jax.shard_map(
        functools.partial(local, mesh.shape["sec"], mesh.shape["rows"]),
        mesh=mesh,
        in_specs=placed,
        out_specs=(
            P("sec", None, "rows", None, None),
            P("sec", None, "rows", None, None),
            P("sec", "rows", None),
        ),
        check_vma=False,
    )
```

```python
import functools

import jax
import jax.numpy as jnp
from jax import lax
from jax.experimental import pallas as pl
from jax.experimental.pallas import tpu as pltpu
from jax.sharding import PartitionSpec as P

MESH = pl.DeviceIdType.MESH
F32 = jnp.float32
BF16 = jnp.bfloat16


def sigmoid(value):
    return 0.5 * jnp.tanh(0.5 * value) + 0.5


def silu_slope(value, sig):
    return sig + value * sig * (1.0 - sig)


def shift_cols(value, by, width):
    shaped = value.reshape(-1, width, value.shape[1])
    rolled = pltpu.roll(shaped, by % width, axis=1)
    col = lax.broadcasted_iota(jnp.int32, shaped.shape, 1)
    edge = 0 if by > 0 else width - 1
    return jnp.where(col == edge, 0.0, rolled).reshape(value.shape)


def conv(field, kernel, width):
    pixels, channels = field.shape[0] - 2 * width, field.shape[1]
    stacked = jnp.concatenate([field[a * width : a * width + pixels] for a in range(3)], 1)
    wide = jnp.dot(stacked, kernel, preferred_element_type=F32)
    left, centre, right = (wide[:, b * channels : (b + 1) * channels] for b in range(3))
    return centre + shift_cols(left, 1, width) + shift_cols(right, -1, width)


def all_grads(acc_ref, which, fields, cotans, width):
    pixels, channels = cotans[0].shape
    shifted = []
    for cotan in cotans:
        wide = cotan.astype(F32)
        shifted.append(
            jnp.concatenate(
                [
                    shift_cols(wide, -1, width).astype(BF16),
                    cotan,
                    shift_cols(wide, 1, width).astype(BF16),
                ],
                axis=1,
            )
        )
    shifted = jnp.concatenate(shifted, 0)
    for a in range(3):
        stacked = jnp.concatenate([f[a * width : a * width + pixels] for f in fields], 0)
        term = lax.dot_general(
            stacked, shifted, (((0,), (0,)), ((), ())), preferred_element_type=F32
        )
        for b in range(3):
            start = ((which * 3 + a) * 3 + b) * channels
            acc_ref[start : start + channels] = term[:, b * channels : (b + 1) * channels]


def body(
    S, N, scale,
    streams, cotangents, weights_in, out_streams, out_grads, out_weights,
    taps, turned, first, state, made, edge_a, edge_b, keep_g, keep_f, result, acc, terms, mid, sums, got,
    in_sem, w_sem, first_send, fedge_send, st_send, st_recv, ea_send, ea_recv, eb_send, eb_recv,
    res_send, res_recv, pair_send, pair_recv, rs_send, rs_recv, go,
):
    s, r = lax.axis_index("sec"), lax.axis_index("rows")
    M = S
    rows, width, channels = state.shape[2:]
    chunk = terms.shape[1]
    last_sec = s == S - 1

    def placed(row):
        return 2 * (row // 2) + lax.rem(row + row // 2, 2)

    def sides_of(row):
        above, below = placed(lax.rem(row + N - 1, N)), placed(lax.rem(row + 1, N))
        return ((0, above, row > 0), (1, below, row < N - 1))

    block = placed(r)
    moved_block = block != r
    sides, first_sides = sides_of(block), sides_of(r)
    edge_row = (0, rows - 1)
    lower_sec = lax.rem(s + S - 1, S)
    half, group = lax.rem(r, 2), r // 2
    groups = N // 2
    partner = 2 * group + 1 - half

    def remote(src, dst, send, recv, sec, row):
        return pltpu.make_async_remote_copy(
            src_ref=src, dst_ref=dst, send_sem=send, recv_sem=recv,
            device_id=(sec, row), device_id_type=MESH,
        )

    own = S - 1 - s
    sources = (streams.at[0, 0], cotangents.at[0, 1], streams.at[0, 1], cotangents.at[0, 0])
    loads = [pltpu.make_async_copy(src, first.at[i], in_sem.at[i]) for i, src in enumerate(sources)]
    for load in loads:
        load.start()
    for which in (1, 0):
        for a in range(3):
            for b in range(3):
                rows_a, cols_b = pl.ds(a * channels, channels), pl.ds(b * channels, channels)
                pltpu.make_async_copy(
                    weights_in.at[0, 0, which, a, b], taps.at[which, rows_a, cols_b],
                    w_sem.at[which],
                ).start()

    barrier = pltpu.get_barrier_semaphore()
    pairs = ((group, True), (group - 1, group > 0), (group + 1, group < groups - 1))
    for step in range(1, N):
        pl.semaphore_signal(
            barrier, inc=1, device_id=(s, lax.rem(r + step, N)), device_id_type=MESH
        )
    for pair, there in pairs:
        @pl.when(there)
        def _(pair=pair):
            for step in range(1, S):
                for row in range(2):
                    pl.semaphore_signal(
                        barrier, inc=1, device_id=(lax.rem(s + step, S), 2 * pair + row),
                        device_id_type=MESH,
                    )

    for side, _, there in sides:
        @pl.when(jnp.logical_not(there))
        def _(side=side):
            edge_a[:, side] = jnp.zeros(edge_a.shape[:1] + edge_a.shape[2:], BF16)
            edge_b[:, side] = jnp.zeros(edge_b.shape[:1] + edge_b.shape[2:], BF16)

    for load in loads:
        load.wait()

    stays = last_sec & jnp.logical_not(moved_block)

    @pl.when(stays)
    def _():
        state[0] = first[...]

    def away(row):
        return jnp.logical_not(last_sec & (row == r))

    for side, row, there in first_sides:
        @pl.when(there & last_sec & (row == r))
        def _(side=side):
            for i in range(2):
                edge_a[0, 1 - side, i] = first[i, edge_row[side]]

    near = 1 + (group > 0).astype(jnp.int32) + (group < groups - 1).astype(jnp.int32)
    pl.semaphore_wait(barrier, 2 * (S - 1) * near + N - 1)

    def first_edge(i, side, row):
        return remote(
            first.at[i, edge_row[side]], edge_a.at[own, 1 - side, i],
            fedge_send.at[side, i], ea_recv.at[own, 2 * (1 - side) + i], S - 1, row,
        )

    def first_state(i):
        return remote(
            first.at[i], state.at[own, i], first_send.at[i], st_recv.at[own, i], S - 1, block,
        )

    @pl.when(own >= 2)
    def _():
        pl.semaphore_wait(go, 1)

    for i in range(2):
        for side, row, there in first_sides:
            @pl.when(there & away(row))
            def _(i=i, side=side, row=row):
                first_edge(i, side, row).start()

    @pl.when(jnp.logical_not(stays))
    def _():
        for i in range(4):
            first_state(i).start()

    for which in (1, 0):
        pltpu.make_async_copy(taps.at[which], taps.at[which], w_sem.at[which]).wait()
        for a in range(3):
            for b in range(3):
                turned[which, a * channels : (a + 1) * channels, b * channels : (b + 1) * channels] = (
                    taps[
                        which,
                        (2 - a) * channels : (3 - a) * channels,
                        (2 - b) * channels : (3 - b) * channels,
                    ].T
                )

    def state_copy(m, i):
        return remote(
            made.at[m, i], state.at[m, i], st_send.at[m, i], st_recv.at[m, i], lower_sec, r,
        )

    def result_copy(m, i):
        return remote(
            made.at[m, i], result.at[i], res_send.at[m, i], res_recv.at[i], S - 1 - m, block,
        )

    def edge_a_copy(m, i, side, row):
        return remote(
            made.at[m, i, edge_row[side]], edge_a.at[m, 1 - side, i],
            ea_send.at[m, 2 * side + i], ea_recv.at[m, 2 * (1 - side) + i], lower_sec, row,
        )

    def edge_b_copy(m, i, side, row):
        return remote(
            made.at[m, 2 + i, edge_row[side]], edge_b.at[m, 1 - side, i],
            eb_send.at[m, 2 * side + i], eb_recv.at[m, 2 * (1 - side) + i], s, row,
        )

    def send_on(m, i):
        @pl.when(s > 0)
        def _():
            state_copy(m, i).start()

        @pl.when((s == 0) & ((m < M - 1) | moved_block))
        def _():
            result_copy(m, i).start()

    def rows_of(p):
        return pl.ds(pl.multiple_of(p * chunk, chunk), chunk)

    def pair_copy(k):
        return remote(terms.at[k], mid.at[k], pair_send.at[k], pair_recv.at[k], s, partner)

    def sum_copy(k):
        return remote(
            sums.at[k], got.at[group], rs_send.at[k], rs_recv.at[group], s, 2 * k + half
        )

    def send_pairs(low, count):
        def one(i, carry):
            k = low + lax.rem(group + 1 + i, count)
            terms[k] = acc[rows_of(2 * k + 1 - half)].astype(terms.dtype)
            pair_copy(k).start()
            return carry
        lax.fori_loop(0, count, one, 0)

    def send_sums(low, count):
        def one(i, carry):
            k = low + lax.rem(group + 1 + i, count)
            pair_copy(k).wait_recv()
            total = acc[rows_of(2 * k + half)] + mid[k].astype(F32)

            @pl.when(k == group)
            def _():
                out_weights[0] = total

            @pl.when(k != group)
            def _():
                sums[k] = total.astype(sums.dtype)
                sum_copy(k).start()
            return carry
        lax.fori_loop(0, count, one, 0)

    def flat(value):
        return value.reshape(-1, channels)

    def step(m, carry):
        arrives = jnp.logical_not(stays & (m == 0))

        def await_state(i):
            @pl.when(arrives)
            def _():
                state_copy(m, i).wait_recv()

        def await_edges(copy, i):
            for side, row, there in sides:
                if copy is edge_a_copy:
                    here = last_sec & (m == 0) & (block + 2 * side - 1 == r)
                    there = there & jnp.logical_not(here)

                @pl.when(there)
                def _(side=side, row=row):
                    copy(m, i, 1 - side, row).wait_recv()

        def send_edges(copy, i, ok=True):
            for side, row, there in sides:
                @pl.when(there & ok)
                def _(side=side, row=row):
                    copy(m, i, side, row).start()

        def grads_g():
            crops = range(M)
            all_grads(acc, 1, [keep_g[c] for c in crops], [flat(state[c, 1]) for c in crops], width)
            send_pairs(groups // 2, groups - groups // 2)

        def grads_f():
            crops = range(M)
            all_grads(acc, 0, [keep_f[c] for c in crops], [flat(made[c, 3]) for c in crops], width)
            send_pairs(0, groups // 2)

        last = m == M - 1

        await_edges(edge_a_copy, 0)
        await_state(0)
        y1 = flat(state[m, 0])
        upper = jnp.concatenate([edge_a[m, 0, 0], y1, edge_a[m, 1, 0]], 0)
        upper = upper.astype(F32)
        sig = sigmoid(upper)
        act_g = (upper * sig).astype(BF16)
        slope = silu_slope(upper[width:-width], sig[width:-width])
        keep_g[m] = act_g
        moved = conv(act_g, taps[1], width)
        await_state(2)
        x2 = (flat(state[m, 2]).astype(F32) - moved).astype(BF16)
        made[m, 2] = x2.reshape(rows, width, channels)
        send_edges(edge_b_copy, 0)
        send_on(m, 2)

        @pl.when(last_sec & (m < M - 2))
        def _():
            pl.semaphore_signal(go, inc=1, device_id=(S - 3 - m, block), device_id_type=MESH)

        await_edges(edge_a_copy, 1)
        await_state(1)
        g2 = flat(state[m, 1])
        g2_wide = jnp.concatenate([edge_a[m, 0, 1], g2, edge_a[m, 1, 1]], 0)
        moved = conv(g2_wide, turned[1], width) * slope
        await_state(3)
        carried = (flat(state[m, 3]).astype(F32) + moved).astype(BF16)
        made[m, 3] = carried.reshape(rows, width, channels)
        send_edges(edge_b_copy, 1)
        send_on(m, 3)

        @pl.when(last & (s < 2))
        def _():
            grads_g()

        await_edges(edge_b_copy, 0)
        lower = jnp.concatenate([edge_b[m, 0, 0], x2, edge_b[m, 1, 0]], 0)
        lower = lower.astype(F32)
        sig = sigmoid(lower)
        act_f = (lower * sig).astype(BF16)
        slope = silu_slope(lower[width:-width], sig[width:-width])
        keep_f[m] = act_f

        @pl.when(last & (s == 0))
        def _():
            grads_f()

        x1 = (y1.astype(F32) - conv(act_f, taps[0], width)).astype(BF16)
        made[m, 0] = x1.reshape(rows, width, channels)
        send_edges(edge_a_copy, 0, s > 0)
        send_on(m, 0)

        await_edges(edge_b_copy, 1)
        carried_wide = jnp.concatenate([edge_b[m, 0, 1], carried, edge_b[m, 1, 1]], 0)
        moved = conv(carried_wide, turned[0], width) * slope
        made[m, 1] = (g2.astype(F32) + moved).astype(BF16).reshape(rows, width, channels)
        send_edges(edge_a_copy, 1, s > 0)
        send_on(m, 1)

        @pl.when(last & (s > 1))
        def _():
            grads_g()

        @pl.when(last & (s > 0))
        def _():
            grads_f()

        return carry

    lax.fori_loop(0, M, step, 0)
    send_sums(groups // 2, groups - groups // 2)
    send_sums(0, groups // 2)

    def deliver(source):
        out_streams[0, 0] = source[0]
        out_grads[0, 1] = source[1]
        out_streams[0, 1] = source[2]
        out_grads[0, 0] = source[3]

    @pl.when((s == 0) & jnp.logical_not(moved_block))
    def _():
        deliver(made[M - 1])

    @pl.when((s > 0) | moved_block)
    def _():
        for i in range(4):
            result_copy(0, i).wait_recv()
        deliver(result[...])

    for side, row, there in first_sides:
        @pl.when(there & away(row))
        def _(side=side, row=row):
            for i in range(2):
                first_edge(i, side, row).wait_send()

    @pl.when(jnp.logical_not(stays))
    def _():
        for i in range(4):
            first_state(i).wait_send()

    def drain(m, carry):
        for side, row, there in sides:
            @pl.when(there)
            def _(side=side, row=row):
                for i in range(2):
                    edge_b_copy(m, i, side, row).wait_send()

            @pl.when(there & (s > 0))
            def _(side=side, row=row):
                for i in range(2):
                    edge_a_copy(m, i, side, row).wait_send()

        @pl.when(s > 0)
        def _():
            for i in range(4):
                state_copy(m, i).wait_send()

        @pl.when((s == 0) & ((m < M - 1) | moved_block))
        def _():
            for i in range(4):
                result_copy(m, i).wait_send()
        return carry

    lax.fori_loop(0, M, drain, 0)

    def gather(i, carry):
        k = lax.rem(group + groups - i, groups)
        remote(
            sums.at[k], got.at[k], rs_send.at[k], rs_recv.at[k], s, 2 * k + half
        ).wait_recv()
        out_weights[0] += got[k].astype(F32)
        return carry

    lax.fori_loop(1, groups, gather, 0)
    out_weights[...] = out_weights[...] * scale

    def drain_terms(k, carry):
        pair_copy(k).wait_send()

        @pl.when(k != group)
        def _():
            sum_copy(k).wait_send()
        return carry

    lax.fori_loop(0, groups, drain_terms, 0)


def local(S, N, streams, cotangents, weights):
    mine, _, rows, width, channels = streams.shape
    layers = weights.shape[1]
    assert mine == 1 and layers == 1 and N % 2 == 0
    M = S
    scale = (M * rows * N * width) ** -0.5
    total = 18 * channels
    chunk = total // N
    sent = BF16 if chunk % 16 == 0 else F32
    dma = pltpu.SemaphoreType.DMA
    vmem = pl.BlockSpec(memory_space=pltpu.VMEM)
    shard = (rows, width, channels)
    edge = (2, 2, width, channels)
    return pl.pallas_call(
        functools.partial(body, S, N, scale),
        out_shape=(
            jax.ShapeDtypeStruct(streams.shape, BF16),
            jax.ShapeDtypeStruct(streams.shape, BF16),
            jax.ShapeDtypeStruct((1, chunk, channels), F32),
        ),
        in_specs=[pl.BlockSpec(memory_space=pltpu.HBM)] * 3,
        out_specs=(vmem,) * 3,
        scratch_shapes=[
            pltpu.VMEM((2, 3 * channels, 3 * channels), BF16),
            pltpu.VMEM((2, 3 * channels, 3 * channels), BF16),
            pltpu.VMEM((4,) + shard, BF16),
            pltpu.VMEM((M, 4) + shard, BF16),
            pltpu.VMEM((M, 4) + shard, BF16),
            pltpu.VMEM((M,) + edge, BF16),
            pltpu.VMEM((M,) + edge, BF16),
            pltpu.VMEM((M, (rows + 2) * width, channels), BF16),
            pltpu.VMEM((M, (rows + 2) * width, channels), BF16),
            pltpu.VMEM((4,) + shard, BF16),
            pltpu.VMEM((total, channels), F32),
            pltpu.VMEM((N // 2, chunk, channels), sent),
            pltpu.VMEM((N // 2, chunk, channels), sent),
            pltpu.VMEM((N // 2, chunk, channels), sent),
            pltpu.VMEM((N // 2, chunk, channels), sent),
            dma((4,)), dma((2,)), dma((4,)), dma((2, 2)),
            dma((M, 4)), dma((M, 4)), dma((M, 4)), dma((M, 4)), dma((M, 4)), dma((M, 4)),
            dma((M, 4)), dma((4,)),
            dma((N // 2,)), dma((N // 2,)), dma((N // 2,)), dma((N // 2,)),
            pltpu.SemaphoreType.REGULAR,
        ],
        compiler_params=pltpu.CompilerParams(
            collective_id=0, has_side_effects=True, vmem_limit_bytes=52 * 1024 * 1024
        ),
        cost_estimate=pl.CostEstimate(
            flops=M * 108 * rows * width * channels * channels,
            bytes_accessed=weights.size * 2,
            transcendentals=0,
        ),
    )(streams, cotangents, weights)


def solution(mesh):
    placed = (
        P("sec", None, "rows", None, None),
        P("sec", None, "rows", None, None),
        P("sec", None, None, None, None, None, None),
    )
    return jax.shard_map(
        functools.partial(local, mesh.shape["sec"], mesh.shape["rows"]),
        mesh=mesh,
        in_specs=placed,
        out_specs=(
            P("sec", None, "rows", None, None),
            P("sec", None, "rows", None, None),
            P("sec", "rows", None),
        ),
        check_vma=False,
    )
```

```python
import functools

import jax
import jax.numpy as jnp
from jax import lax
from jax.experimental import pallas as pl
from jax.experimental.pallas import tpu as pltpu
from jax.sharding import PartitionSpec as P

MESH = pl.DeviceIdType.MESH
F32 = jnp.float32
BF16 = jnp.bfloat16


def sigmoid(value):
    return 0.5 * jnp.tanh(0.5 * value) + 0.5


def silu_slope(value, sig):
    return sig + value * sig * (1.0 - sig)


def shift_cols(value, by, width):
    shaped = value.reshape(-1, width, value.shape[1])
    rolled = pltpu.roll(shaped, by % width, axis=1)
    col = lax.broadcasted_iota(jnp.int32, shaped.shape, 1)
    edge = 0 if by > 0 else width - 1
    return jnp.where(col == edge, 0.0, rolled).reshape(value.shape)


def conv(field, kernel, width):
    pixels, channels = field.shape[0] - 2 * width, field.shape[1]
    stacked = jnp.concatenate([field[a * width : a * width + pixels] for a in range(3)], 1)
    wide = jnp.dot(stacked, kernel, preferred_element_type=F32)
    left, centre, right = (wide[:, b * channels : (b + 1) * channels] for b in range(3))
    return centre + shift_cols(left, 1, width) + shift_cols(right, -1, width)


def all_grads(acc_ref, which, fields, cotans, width):
    pixels, channels = cotans[0].shape
    shifted = []
    for cotan in cotans:
        wide = cotan.astype(F32)
        shifted.append(
            jnp.concatenate(
                [
                    shift_cols(wide, -1, width).astype(BF16),
                    cotan,
                    shift_cols(wide, 1, width).astype(BF16),
                ],
                axis=1,
            )
        )
    shifted = jnp.concatenate(shifted, 0)
    for a in range(3):
        stacked = jnp.concatenate([f[a * width : a * width + pixels] for f in fields], 0)
        term = lax.dot_general(
            stacked, shifted, (((0,), (0,)), ((), ())), preferred_element_type=F32
        )
        for b in range(3):
            start = ((which * 3 + a) * 3 + b) * channels
            acc_ref[start : start + channels] = term[:, b * channels : (b + 1) * channels]


def body(
    S, N, scale,
    streams, cotangents, weights_in, out_streams, out_grads, out_weights,
    taps, turned, first, state, made, edge_a, edge_b, keep_g, keep_f, result, acc, terms, mid, sums, got,
    in_sem, w_sem, first_send, fedge_send, st_send, st_recv, ea_send, ea_recv, eb_send, eb_recv,
    res_send, res_recv, pair_send, pair_recv, rs_send, rs_recv, go,
):
    s, r = lax.axis_index("sec"), lax.axis_index("rows")
    M = S
    rows, width, channels = state.shape[2:]
    chunk = terms.shape[1]
    last_sec = s == S - 1

    def placed(row):
        return 2 * (row // 2) + lax.rem(row + row // 2, 2)

    def sides_of(row):
        above, below = placed(lax.rem(row + N - 1, N)), placed(lax.rem(row + 1, N))
        return ((0, above, row > 0), (1, below, row < N - 1))

    block = placed(r)
    moved_block = block != r
    sides, first_sides = sides_of(block), sides_of(r)
    edge_row = (0, rows - 1)
    lower_sec = lax.rem(s + S - 1, S)
    half, group = lax.rem(r, 2), r // 2
    groups = N // 2
    partner = 2 * group + 1 - half

    def remote(src, dst, send, recv, sec, row):
        return pltpu.make_async_remote_copy(
            src_ref=src, dst_ref=dst, send_sem=send, recv_sem=recv,
            device_id=(sec, row), device_id_type=MESH,
        )

    own = S - 1 - s
    sources = (streams.at[0, 0], cotangents.at[0, 1], streams.at[0, 1], cotangents.at[0, 0])
    loads = [pltpu.make_async_copy(src, first.at[i], in_sem.at[i]) for i, src in enumerate(sources)]
    for load in loads:
        load.start()
    for which in (1, 0):
        for a in range(3):
            for b in range(3):
                rows_a, cols_b = pl.ds(a * channels, channels), pl.ds(b * channels, channels)
                pltpu.make_async_copy(
                    weights_in.at[0, 0, which, a, b], taps.at[which, rows_a, cols_b],
                    w_sem.at[which],
                ).start()

    barrier = pltpu.get_barrier_semaphore()
    pairs = ((group, True), (group - 1, group > 0), (group + 1, group < groups - 1))
    for step in range(1, N):
        pl.semaphore_signal(
            barrier, inc=1, device_id=(s, lax.rem(r + step, N)), device_id_type=MESH
        )
    for pair, there in pairs:
        @pl.when(there)
        def _(pair=pair):
            for step in range(1, S):
                for row in range(2):
                    pl.semaphore_signal(
                        barrier, inc=1, device_id=(lax.rem(s + step, S), 2 * pair + row),
                        device_id_type=MESH,
                    )

    for side, _, there in sides:
        @pl.when(jnp.logical_not(there))
        def _(side=side):
            edge_a[:, side] = jnp.zeros(edge_a.shape[:1] + edge_a.shape[2:], BF16)
            edge_b[:, side] = jnp.zeros(edge_b.shape[:1] + edge_b.shape[2:], BF16)

    for load in loads:
        load.wait()

    stays = last_sec & jnp.logical_not(moved_block)

    @pl.when(stays)
    def _():
        state[0] = first[...]

    def away(row):
        return jnp.logical_not(last_sec & (row == r))

    for side, row, there in first_sides:
        @pl.when(there & last_sec & (row == r))
        def _(side=side):
            for i in range(2):
                edge_a[0, 1 - side, i] = first[i, edge_row[side]]

    near = 1 + (group > 0).astype(jnp.int32) + (group < groups - 1).astype(jnp.int32)
    pl.semaphore_wait(barrier, 2 * (S - 1) * near + N - 1)

    def first_edge(i, side, row):
        return remote(
            first.at[i, edge_row[side]], edge_a.at[own, 1 - side, i],
            fedge_send.at[side, i], ea_recv.at[own, 2 * (1 - side) + i], S - 1, row,
        )

    def first_state(i):
        return remote(
            first.at[i], state.at[own, i], first_send.at[i], st_recv.at[own, i], S - 1, block,
        )

    @pl.when(own >= 2)
    def _():
        pl.semaphore_wait(go, 1)

    for i in range(2):
        for side, row, there in first_sides:
            @pl.when(there & away(row))
            def _(i=i, side=side, row=row):
                first_edge(i, side, row).start()

    @pl.when(jnp.logical_not(stays))
    def _():
        for i in range(4):
            first_state(i).start()

    for which in (1, 0):
        pltpu.make_async_copy(taps.at[which], taps.at[which], w_sem.at[which]).wait()
        for a in range(3):
            for b in range(3):
                turned[which, a * channels : (a + 1) * channels, b * channels : (b + 1) * channels] = (
                    taps[
                        which,
                        (2 - a) * channels : (3 - a) * channels,
                        (2 - b) * channels : (3 - b) * channels,
                    ].T
                )

    def state_copy(m, i):
        return remote(
            made.at[m, i], state.at[m, i], st_send.at[m, i], st_recv.at[m, i], lower_sec, r,
        )

    def result_copy(m, i):
        return remote(
            made.at[m, i], result.at[i], res_send.at[m, i], res_recv.at[i], S - 1 - m, block,
        )

    def edge_a_copy(m, i, side, row):
        return remote(
            made.at[m, i, edge_row[side]], edge_a.at[m, 1 - side, i],
            ea_send.at[m, 2 * side + i], ea_recv.at[m, 2 * (1 - side) + i], lower_sec, row,
        )

    def edge_b_copy(m, i, side, row):
        return remote(
            made.at[m, 2 + i, edge_row[side]], edge_b.at[m, 1 - side, i],
            eb_send.at[m, 2 * side + i], eb_recv.at[m, 2 * (1 - side) + i], s, row,
        )

    def send_on(m, i):
        @pl.when(s > 0)
        def _():
            state_copy(m, i).start()

        @pl.when((s == 0) & ((m < M - 1) | moved_block))
        def _():
            result_copy(m, i).start()

    def rows_of(p):
        return pl.ds(pl.multiple_of(p * chunk, chunk), chunk)

    def pair_copy(k):
        return remote(terms.at[k], mid.at[k], pair_send.at[k], pair_recv.at[k], s, partner)

    def sum_copy(k):
        return remote(
            sums.at[k], got.at[group], rs_send.at[k], rs_recv.at[group], s, 2 * k + half
        )

    def send_pairs(low, count):
        def one(i, carry):
            k = low + lax.rem(group + 1 + i, count)
            terms[k] = acc[rows_of(2 * k + 1 - half)].astype(terms.dtype)
            pair_copy(k).start()
            return carry
        lax.fori_loop(0, count, one, 0)

    def send_sums(low, count):
        def one(i, carry):
            k = low + lax.rem(group + 1 + i, count)
            pair_copy(k).wait_recv()
            total = acc[rows_of(2 * k + half)] + mid[k].astype(F32)

            @pl.when(k == group)
            def _():
                out_weights[0] = total

            @pl.when(k != group)
            def _():
                sums[k] = total.astype(sums.dtype)
                sum_copy(k).start()
            return carry
        lax.fori_loop(0, count, one, 0)

    def flat(value):
        return value.reshape(-1, channels)

    def step(m, carry):
        arrives = jnp.logical_not(stays & (m == 0))

        def await_state(i):
            @pl.when(arrives)
            def _():
                state_copy(m, i).wait_recv()

        def await_edges(copy, i):
            for side, row, there in sides:
                if copy is edge_a_copy:
                    here = last_sec & (m == 0) & (block + 2 * side - 1 == r)
                    there = there & jnp.logical_not(here)

                @pl.when(there)
                def _(side=side, row=row):
                    copy(m, i, 1 - side, row).wait_recv()

        def send_edges(copy, i, ok=True):
            for side, row, there in sides:
                @pl.when(there & ok)
                def _(side=side, row=row):
                    copy(m, i, side, row).start()

        def grads_g():
            crops = range(M)
            all_grads(acc, 1, [keep_g[c] for c in crops], [flat(state[c, 1]) for c in crops], width)
            send_pairs(groups // 2, groups - groups // 2)

        def grads_f():
            crops = range(M)
            all_grads(acc, 0, [keep_f[c] for c in crops], [flat(made[c, 3]) for c in crops], width)
            send_pairs(0, groups // 2)

        last = m == M - 1

        await_edges(edge_a_copy, 0)
        await_state(0)
        y1 = flat(state[m, 0])
        upper = jnp.concatenate([edge_a[m, 0, 0], y1, edge_a[m, 1, 0]], 0)
        upper = upper.astype(F32)
        sig = sigmoid(upper)
        act_g = (upper * sig).astype(BF16)
        slope = silu_slope(upper[width:-width], sig[width:-width])
        keep_g[m] = act_g
        moved = conv(act_g, taps[1], width)
        await_state(2)
        x2 = (flat(state[m, 2]).astype(F32) - moved).astype(BF16)
        made[m, 2] = x2.reshape(rows, width, channels)
        send_edges(edge_b_copy, 0)
        send_on(m, 2)

        @pl.when(last_sec & (m < M - 2))
        def _():
            pl.semaphore_signal(go, inc=1, device_id=(S - 3 - m, block), device_id_type=MESH)

        await_edges(edge_a_copy, 1)
        await_state(1)
        g2 = flat(state[m, 1])

        @pl.when(last & (s < 2))
        def _():
            grads_g()

        g2_wide = jnp.concatenate([edge_a[m, 0, 1], g2, edge_a[m, 1, 1]], 0)
        moved = conv(g2_wide, turned[1], width) * slope
        await_state(3)
        carried = (flat(state[m, 3]).astype(F32) + moved).astype(BF16)
        made[m, 3] = carried.reshape(rows, width, channels)
        send_edges(edge_b_copy, 1)
        send_on(m, 3)

        await_edges(edge_b_copy, 0)
        lower = jnp.concatenate([edge_b[m, 0, 0], x2, edge_b[m, 1, 0]], 0)
        lower = lower.astype(F32)
        sig = sigmoid(lower)
        act_f = (lower * sig).astype(BF16)
        slope = silu_slope(lower[width:-width], sig[width:-width])
        keep_f[m] = act_f

        @pl.when(last & (s == 0))
        def _():
            grads_f()

        x1 = (y1.astype(F32) - conv(act_f, taps[0], width)).astype(BF16)
        made[m, 0] = x1.reshape(rows, width, channels)
        send_edges(edge_a_copy, 0, s > 0)
        send_on(m, 0)

        await_edges(edge_b_copy, 1)
        carried_wide = jnp.concatenate([edge_b[m, 0, 1], carried, edge_b[m, 1, 1]], 0)
        moved = conv(carried_wide, turned[0], width) * slope
        made[m, 1] = (g2.astype(F32) + moved).astype(BF16).reshape(rows, width, channels)
        send_edges(edge_a_copy, 1, s > 0)
        send_on(m, 1)

        @pl.when(last & (s > 1))
        def _():
            grads_g()

        @pl.when(last & (s > 0))
        def _():
            grads_f()

        return carry

    lax.fori_loop(0, M, step, 0)
    send_sums(groups // 2, groups - groups // 2)
    send_sums(0, groups // 2)

    def deliver(source):
        out_streams[0, 0] = source[0]
        out_grads[0, 1] = source[1]
        out_streams[0, 1] = source[2]
        out_grads[0, 0] = source[3]

    @pl.when((s == 0) & jnp.logical_not(moved_block))
    def _():
        deliver(made[M - 1])

    @pl.when((s > 0) | moved_block)
    def _():
        for i in range(4):
            result_copy(0, i).wait_recv()
        deliver(result[...])

    for side, row, there in first_sides:
        @pl.when(there & away(row))
        def _(side=side, row=row):
            for i in range(2):
                first_edge(i, side, row).wait_send()

    @pl.when(jnp.logical_not(stays))
    def _():
        for i in range(4):
            first_state(i).wait_send()

    def drain(m, carry):
        for side, row, there in sides:
            @pl.when(there)
            def _(side=side, row=row):
                for i in range(2):
                    edge_b_copy(m, i, side, row).wait_send()

            @pl.when(there & (s > 0))
            def _(side=side, row=row):
                for i in range(2):
                    edge_a_copy(m, i, side, row).wait_send()

        @pl.when(s > 0)
        def _():
            for i in range(4):
                state_copy(m, i).wait_send()

        @pl.when((s == 0) & ((m < M - 1) | moved_block))
        def _():
            for i in range(4):
                result_copy(m, i).wait_send()
        return carry

    lax.fori_loop(0, M, drain, 0)

    def gather(i, carry):
        k = lax.rem(group + groups - i, groups)
        remote(
            sums.at[k], got.at[k], rs_send.at[k], rs_recv.at[k], s, 2 * k + half
        ).wait_recv()
        out_weights[0] += got[k].astype(F32)
        return carry

    lax.fori_loop(1, groups, gather, 0)
    out_weights[...] = out_weights[...] * scale

    def drain_terms(k, carry):
        pair_copy(k).wait_send()

        @pl.when(k != group)
        def _():
            sum_copy(k).wait_send()
        return carry

    lax.fori_loop(0, groups, drain_terms, 0)


def local(S, N, streams, cotangents, weights):
    mine, _, rows, width, channels = streams.shape
    layers = weights.shape[1]
    assert mine == 1 and layers == 1 and N % 2 == 0
    M = S
    scale = (M * rows * N * width) ** -0.5
    total = 18 * channels
    chunk = total // N
    sent = BF16 if chunk % 16 == 0 else F32
    dma = pltpu.SemaphoreType.DMA
    vmem = pl.BlockSpec(memory_space=pltpu.VMEM)
    shard = (rows, width, channels)
    edge = (2, 2, width, channels)
    return pl.pallas_call(
        functools.partial(body, S, N, scale),
        out_shape=(
            jax.ShapeDtypeStruct(streams.shape, BF16),
            jax.ShapeDtypeStruct(streams.shape, BF16),
            jax.ShapeDtypeStruct((1, chunk, channels), F32),
        ),
        in_specs=[pl.BlockSpec(memory_space=pltpu.HBM)] * 3,
        out_specs=(vmem,) * 3,
        scratch_shapes=[
            pltpu.VMEM((2, 3 * channels, 3 * channels), BF16),
            pltpu.VMEM((2, 3 * channels, 3 * channels), BF16),
            pltpu.VMEM((4,) + shard, BF16),
            pltpu.VMEM((M, 4) + shard, BF16),
            pltpu.VMEM((M, 4) + shard, BF16),
            pltpu.VMEM((M,) + edge, BF16),
            pltpu.VMEM((M,) + edge, BF16),
            pltpu.VMEM((M, (rows + 2) * width, channels), BF16),
            pltpu.VMEM((M, (rows + 2) * width, channels), BF16),
            pltpu.VMEM((4,) + shard, BF16),
            pltpu.VMEM((total, channels), F32),
            pltpu.VMEM((N // 2, chunk, channels), sent),
            pltpu.VMEM((N // 2, chunk, channels), sent),
            pltpu.VMEM((N // 2, chunk, channels), sent),
            pltpu.VMEM((N // 2, chunk, channels), sent),
            dma((4,)), dma((2,)), dma((4,)), dma((2, 2)),
            dma((M, 4)), dma((M, 4)), dma((M, 4)), dma((M, 4)), dma((M, 4)), dma((M, 4)),
            dma((M, 4)), dma((4,)),
            dma((N // 2,)), dma((N // 2,)), dma((N // 2,)), dma((N // 2,)),
            pltpu.SemaphoreType.REGULAR,
        ],
        compiler_params=pltpu.CompilerParams(
            collective_id=0, has_side_effects=True, vmem_limit_bytes=52 * 1024 * 1024
        ),
        cost_estimate=pl.CostEstimate(
            flops=M * 108 * rows * width * channels * channels,
            bytes_accessed=weights.size * 2,
            transcendentals=0,
        ),
    )(streams, cotangents, weights)


def solution(mesh):
    placed = (
        P("sec", None, "rows", None, None),
        P("sec", None, "rows", None, None),
        P("sec", None, None, None, None, None, None),
    )
    return jax.shard_map(
        functools.partial(local, mesh.shape["sec"], mesh.shape["rows"]),
        mesh=mesh,
        in_specs=placed,
        out_specs=(
            P("sec", None, "rows", None, None),
            P("sec", None, "rows", None, None),
            P("sec", "rows", None),
        ),
        check_vma=False,
    )
```
